32 devices in a mesh: groups: 2 (over y), space: 4 (over x, core), filt: 4 (over z).
Axes of the slice: x: 2, y: 2, z: 4, core: 2. Of those that a mesh axis runs over, the one named last changes fastest.
Arguments:
- volume: bfloat16 [64, 16, 32, 512], P('filt', ('groups', 'space')), parts along dimension 1, may hold values from -6 to 6
- conv_weight: bfloat16 [3, 3, 3, 4096], replicated, may hold values from -0.15625 to 0.15625
- down_weight: bfloat16 [3, 3, 3, 8192], replicated, may hold values from -0.15625 to 0.15625
Outputs:
- coarse: bfloat16 [128, 8, 16, 256], P(None, ('groups', 'space'), 'filt'), parts along dimension 1
The draws below stay inside these ranges and needn't reach their ends.
There are 2 independent parts, one for each index of `groups`. The reference program is written for one: setup_inputs(seed, part) draws one part's arguments, and reference() takes and returns one part's arrays. A program takes and returns all parts, laid end to end along the dimension named above; an argument that names none is the same for every part. Nothing has to cross between parts.
All inputs are finite; a program needn't handle non-finite values.
Results may differ from the reference program's by a relative error of at most 0.0049.
Values may be sent and summed in bfloat16 or wider, within the bound.
No kernel may reach another device: no remote copies, remote signals or barrier semaphores. Data moves between devices by JAX's collectives and lax.ppermute only.
A program may use at most 128 MiB of HBM per device.

```python
import jax
import jax.numpy as jnp
from jax import lax

C = 64
C2 = 128
Y = 32
X = 512
ZT = 8


def levels(key, shape, cuts, low, top_value):
    level, own = 1.0, jax.random.fold_in(key, 6)
    for dim, shards_of in cuts:
        heights = jnp.exp(jax.random.uniform(jax.random.fold_in(own, dim), (shards_of,), jnp.float32, low / len(cuts), top_value / len(cuts)))
        level = level * jnp.repeat(heights, shape[dim] // shards_of).reshape([-1 if axis == dim else 1 for axis in range(len(shape))])
    return level


def noise(own_key, dims, scale, bound, shards=(), held_as=jnp.bfloat16):
    gain = levels(own_key, dims, shards, -0.22, 0.18) if shards else 1.0
    values = jax.random.normal(own_key, dims, jnp.float32) * scale * gain
    return jnp.minimum(jnp.maximum(values, -bound), bound).astype(held_as)


def setup_inputs(seed: int = 0, part: int = 0) -> dict:
    streams_of = jax.random.split(jax.random.key(seed), 4)
    part_splits = jax.random.split(jax.random.fold_in(streams_of[3], part), 4)
    volume = noise(part_splits[0], (C, ZT, Y, X), 1.0, 6.0, ((0, 4), (1, 4)))
    conv_weight = noise(streams_of[1], (3, 3, 3, C * C), (C * 27) ** -0.5, 0.15625)
    down_weight = noise(streams_of[2], (3, 3, 3, C2 * C), (C * 27) ** -0.5, 0.15625)
    return dict(volume=volume, conv_weight=conv_weight, down_weight=down_weight)


negative_slope = 0.01


def unflatten(weight, in_count):
    out_count = weight.shape[3] // in_count
    shaped = weight.reshape(3, 3, 3, out_count, in_count)
    return jnp.transpose(shaped, (3, 4, 0, 1, 2))


def convolve(field, kernel, strides, padding):
    result = lax.conv_general_dilated(field.astype(jnp.float32)[None], kernel.astype(jnp.float32), strides, padding, dimension_numbers=("NCDHW", "OIDHW", "NCDHW"), precision=lax.Precision.HIGHEST, preferred_element_type=jnp.float32)
    return result[0]


def reference(volume, conv_weight, down_weight):
    in_count = volume.shape[0]
    feature = convolve(volume, unflatten(conv_weight, in_count), (1, 1, 1), ((1, 1), (1, 1), (1, 1)))
    hidden = jnp.where(feature > 0, feature, negative_slope * feature).astype(jnp.bfloat16)
    coarse = convolve(hidden, unflatten(down_weight, in_count), (2, 2, 2), ((1, 0), (1, 0), (1, 0)))
    return coarse.astype(jnp.bfloat16)
```

```python
import functools

import jax
import jax.numpy as jnp
from jax import lax
from jax.experimental import pallas as pl
from jax.experimental.pallas import tpu as pltpu
from jax.sharding import PartitionSpec as P

C = 64
C2 = 128
negative_slope = 0.01
VMEM_LIMIT = 56 * 1024 * 1024


def split_matrix(width):
    half = width // 2
    source = lax.broadcasted_iota(jnp.int32, (width, width), 0)
    column = lax.broadcasted_iota(jnp.int32, (width, width), 1)
    wanted = jnp.where(column < half, 2 * column, 2 * (column - half) + 1)
    return jnp.where(source == wanted, 1.0, 0.0).astype(jnp.bfloat16)


def gather_kernel(*refs):
    order_ref, pieces, out_ref = refs[0], refs[1:-1], refs[-1]
    rows, planes, count, width = pieces[0].shape
    split = split_matrix(width)
    for d, piece in enumerate(pieces):
        flat = piece[...].reshape(rows * planes * count, width)
        moved = jnp.dot(flat, split, preferred_element_type=jnp.float32)
        at = pl.multiple_of(order_ref[d] * count, count)
        out_ref[:, :, pl.ds(at, count), :] = moved.astype(jnp.bfloat16).reshape(
            rows, planes, count, width
        )


def conv_kernel(edge_ref, low_ref, own_ref, high_ref, first_ref, second_ref, out_ref, taps_ref, hid_ref):
    rows = own_ref.shape[0]
    half = own_ref.shape[3] // 2
    hid_rows = rows - 2
    lane = lax.broadcasted_iota(jnp.int32, (C, half), 1)
    for r in range(rows):
        for p in range(5):
            if p < 2:
                cell = low_ref[r, p]
            elif p < 4:
                cell = own_ref[r, p - 2]
            else:
                cell = high_ref[r, 0]
            even, odd = cell[:, :half], cell[:, half:]
            zero = jnp.zeros((C, half), jnp.float32)
            before = jnp.where(lane == 0, zero, pltpu.roll(odd.astype(jnp.float32), 1, 1))
            after = jnp.where(lane == half - 1, zero, pltpu.roll(even.astype(jnp.float32), half - 1, 1))
            base = r * 4 * C
            taps_ref[p, pl.ds(base, C), :] = before.astype(jnp.bfloat16)
            taps_ref[p, pl.ds(base + C, C), :] = even
            taps_ref[p, pl.ds(base + 2 * C, C), :] = odd
            taps_ref[p, pl.ds(base + 3 * C, C), :] = after.astype(jnp.bfloat16)
    size = 2 * C
    for y in range(hid_rows):
        total = [None] * 3
        for p in range(5):
            z_low, z_high = max(0, p - 2), min(2, p)
            first = 2 - (p - z_low)
            weight = first_ref[pl.ds(first * size, (z_high - z_low + 1) * size), :]
            part = jnp.dot(
                weight, taps_ref[p, pl.ds(y * 4 * C, 12 * C), :], preferred_element_type=jnp.float32
            )
            for z in range(z_low, z_high + 1):
                piece = part[(z - z_low) * size : (z - z_low + 1) * size]
                total[z] = piece if total[z] is None else total[z] + piece
        for z in range(3):
            value = total[z]
            value = jnp.where(value > 0, value, negative_slope * value)
            if z == 0:
                value = jnp.where(edge_ref[0] > 0, value, 0.0)
            if y == 0:
                value = jnp.where(edge_ref[1] > 0, value, 0.0)
            value = value.astype(jnp.bfloat16)
            odd = value[C:]
            before = jnp.where(lane == 0, 0.0, pltpu.roll(odd.astype(jnp.float32), 1, 1))
            base = (y * 3 + z) * 3 * C
            hid_ref[pl.ds(base, C), :] = before.astype(jnp.bfloat16)
            hid_ref[pl.ds(base + C, 2 * C), :] = value
    for y in range(out_ref.shape[0]):
        out_ref[y] = jnp.dot(
            second_ref[...], hid_ref[pl.ds(2 * y * 9 * C, 27 * C), :], preferred_element_type=jnp.float32
        ).astype(jnp.bfloat16)


def first_weights(conv_weight):
    shaped = jnp.transpose(conv_weight.reshape(3, 3, 3, C, C), (0, 3, 1, 2, 4))
    shaped = shaped[::-1]
    even = jnp.pad(shaped, ((0, 0), (0, 0), (0, 0), (0, 1), (0, 0)))
    odd = jnp.pad(shaped, ((0, 0), (0, 0), (0, 0), (1, 0), (0, 0)))
    return jnp.stack([even, odd], axis=1).reshape(3 * 2 * C, 12 * C)


def second_weights(down_weight):
    shaped = down_weight.reshape(3, 3, 3, C2, C)
    return jnp.transpose(shaped, (3, 1, 0, 2, 4)).reshape(C2, 27 * C)


def shifted(block, axis, by):
    count = lax.axis_size(axis)
    return lax.ppermute(block, axis, [(i, i + by) for i in range(count) if 0 <= i + by < count])


def local(volume, conv_weight, down_weight):
    bands = lax.axis_size("filt")
    me = lax.axis_index("filt")
    count, planes, all_rows, width = volume.shape
    band = all_rows // bands
    window = band + 3
    field = jnp.transpose(volume, (2, 1, 0, 3))
    field = jnp.pad(field, ((2, 1), (0, 0), (0, 0), (0, 0)))
    vmem = pl.BlockSpec(memory_space=pltpu.VMEM)
    smem = pl.BlockSpec(memory_space=pltpu.SMEM)
    params = pltpu.CompilerParams(vmem_limit_bytes=VMEM_LIMIT)
    if count % 16 == 0:
        pieces = []
        for d in range(bands):
            target = lax.rem(me + d, bands)
            piece = lax.dynamic_slice_in_dim(field, target * band, window, 0)
            if d:
                piece = lax.ppermute(piece, "filt", [(i, (i + d) % bands) for i in range(bands)])
            pieces.append(piece)
        order = lax.rem(me - jnp.arange(bands, dtype=jnp.int32) + bands, bands)
    else:
        sent = jnp.stack([field[t * band : t * band + window] for t in range(bands)])
        got = lax.all_to_all(sent, "filt", split_axis=0, concat_axis=0, tiled=True)
        pieces = [jnp.transpose(got, (1, 2, 0, 3, 4)).reshape(window, planes, C, width)]
        order = jnp.zeros((1,), jnp.int32)
    own = pl.pallas_call(
        gather_kernel,
        out_shape=jax.ShapeDtypeStruct((window, planes, C, width), jnp.bfloat16),
        in_specs=[smem] + [vmem] * len(pieces),
        out_specs=vmem,
        compiler_params=params,
    )(order, *pieces)
    low = shifted(own, "space", 1)
    high = shifted(own[:, :1], "space", -1)
    edge = jnp.stack([lax.axis_index("space"), me]).astype(jnp.int32)
    coarse = pl.pallas_call(
        conv_kernel,
        out_shape=jax.ShapeDtypeStruct((band // 2, C2, width // 2), jnp.bfloat16),
        in_specs=[smem] + [vmem] * 5,
        out_specs=vmem,
        scratch_shapes=[
            pltpu.VMEM((5, window * 4 * C, width // 2), jnp.bfloat16),
            pltpu.VMEM(((band + 1) * 9 * C, width // 2), jnp.bfloat16),
        ],
        compiler_params=params,
    )(edge, low, own, high, first_weights(conv_weight), second_weights(down_weight))
    return jnp.transpose(coarse, (1, 0, 2))[:, None]


def solution(mesh):
    return jax.shard_map(
        local,
        mesh=mesh,
        in_specs=(P("filt", ("groups", "space"), None, None), P(), P()),
        out_specs=P(None, ("groups", "space"), "filt", None),
        check_vma=False,
    )
```

```python
import functools

import jax
import jax.numpy as jnp
from jax import lax
from jax.experimental import pallas as pl
from jax.experimental.pallas import tpu as pltpu
from jax.sharding import PartitionSpec as P

C = 64
C2 = 128
negative_slope = 0.01
VMEM_LIMIT = 56 * 1024 * 1024


def split_matrix(width):
    half = width // 2
    source = lax.broadcasted_iota(jnp.int32, (width, width), 0)
    column = lax.broadcasted_iota(jnp.int32, (width, width), 1)
    wanted = jnp.where(column < half, 2 * column, 2 * (column - half) + 1)
    return jnp.where(source == wanted, 1.0, 0.0).astype(jnp.bfloat16)


def gather_kernel(*refs):
    order_ref, pieces, out_ref = refs[0], refs[1:-1], refs[-1]
    rows, planes, count, width = pieces[0].shape
    split = split_matrix(width)
    for d, piece in enumerate(pieces):
        flat = piece[...].reshape(rows * planes * count, width)
        moved = jnp.dot(flat, split, preferred_element_type=jnp.float32)
        at = pl.multiple_of(order_ref[d] * count, count)
        out_ref[:, :, pl.ds(at, count), :] = moved.astype(jnp.bfloat16).reshape(
            rows, planes, count, width
        )


def conv_kernel(rows, *refs):
    edge_ref, first_ref, second_ref = refs[:3]
    blocks, (out_ref, taps_ref, hid_ref) = refs[3:-3], refs[-3:]
    half = out_ref.shape[2]
    lane = lax.broadcasted_iota(jnp.int32, (C, half), 1)
    for r, (chunk, at) in enumerate(rows):
        low_ref, own_ref, high_ref = blocks[3 * chunk : 3 * chunk + 3]
        for p in range(5):
            if p < 2:
                cell = low_ref[at, p]
            elif p < 4:
                cell = own_ref[at, p - 2]
            else:
                cell = high_ref[at, 0]
            even, odd = cell[:, :half], cell[:, half:]
            before = jnp.where(lane == 0, 0.0, pltpu.roll(odd.astype(jnp.float32), 1, 1))
            after = jnp.where(lane == half - 1, 0.0, pltpu.roll(even.astype(jnp.float32), half - 1, 1))
            base = r * 4 * C
            taps_ref[p, pl.ds(base, C), :] = before.astype(jnp.bfloat16)
            taps_ref[p, pl.ds(base + C, C), :] = even
            taps_ref[p, pl.ds(base + 2 * C, C), :] = odd
            taps_ref[p, pl.ds(base + 3 * C, C), :] = after.astype(jnp.bfloat16)
    size = 2 * C
    for y in range(len(rows) - 2):
        total = [None] * 3
        for p in range(5):
            z_low, z_high = max(0, p - 2), min(2, p)
            first = 2 - (p - z_low)
            weight = first_ref[pl.ds(first * size, (z_high - z_low + 1) * size), :]
            part = jnp.dot(
                weight, taps_ref[p, pl.ds(y * 4 * C, 12 * C), :], preferred_element_type=jnp.float32
            )
            for z in range(z_low, z_high + 1):
                piece = part[(z - z_low) * size : (z - z_low + 1) * size]
                total[z] = piece if total[z] is None else total[z] + piece
        for z in range(3):
            value = total[z]
            value = jnp.where(value > 0, value, negative_slope * value)
            if z == 0:
                value = jnp.where(edge_ref[0] > 0, value, 0.0)
            if y == 0:
                value = jnp.where(edge_ref[1] > 0, value, 0.0)
            value = value.astype(jnp.bfloat16)
            before = jnp.where(lane == 0, 0.0, pltpu.roll(value[C:].astype(jnp.float32), 1, 1))
            base = (y * 3 + z) * 3 * C
            hid_ref[pl.ds(base, C), :] = before.astype(jnp.bfloat16)
            hid_ref[pl.ds(base + C, 2 * C), :] = value
    for y in range(out_ref.shape[0]):
        out_ref[y] = jnp.dot(
            second_ref[...], hid_ref[pl.ds(2 * y * 9 * C, 27 * C), :], preferred_element_type=jnp.float32
        ).astype(jnp.bfloat16)


def first_weights(conv_weight):
    shaped = jnp.transpose(conv_weight.reshape(3, 3, 3, C, C), (0, 3, 1, 2, 4))
    shaped = shaped[::-1]
    even = jnp.pad(shaped, ((0, 0), (0, 0), (0, 0), (0, 1), (0, 0)))
    odd = jnp.pad(shaped, ((0, 0), (0, 0), (0, 0), (1, 0), (0, 0)))
    return jnp.stack([even, odd], axis=1).reshape(3 * 2 * C, 12 * C)


def second_weights(down_weight):
    shaped = down_weight.reshape(3, 3, 3, C2, C)
    return jnp.transpose(shaped, (3, 1, 0, 2, 4)).reshape(C2, 27 * C)


def shifted(block, axis, by):
    count = lax.axis_size(axis)
    return lax.ppermute(block, axis, [(i, i + by) for i in range(count) if 0 <= i + by < count])


def after(value, *others):
    return lax.optimization_barrier((value, *others))[0]


def chunks_of(band):
    window = band + 3
    if band < 8:
        return [(0, window)]
    return [(0, 5), (5, window - 2), (window - 2, window)]


def local(volume, conv_weight, down_weight):
    bands = lax.axis_size("filt")
    me = lax.axis_index("filt")
    count, planes, all_rows, width = volume.shape
    band = all_rows // bands
    chunks = chunks_of(band)
    field = jnp.transpose(volume, (2, 1, 0, 3))
    field = jnp.pad(field, ((2, 1), (0, 0), (0, 0), (0, 0)))
    vmem = pl.BlockSpec(memory_space=pltpu.VMEM)
    smem = pl.BlockSpec(memory_space=pltpu.SMEM)
    params = pltpu.CompilerParams(vmem_limit_bytes=VMEM_LIMIT)
    first, second = first_weights(conv_weight), second_weights(down_weight)
    space = lax.axis_index("space")

    travelled = []
    for low, high in chunks:
        pieces = []
        if count % 16 == 0:
            for d in range(bands):
                target = lax.rem(me + d, bands)
                piece = lax.dynamic_slice_in_dim(field, target * band + low, high - low, 0)
                if d:
                    if travelled:
                        piece = after(piece, travelled[-1][d])
                    piece = lax.ppermute(piece, "filt", [(i, (i + d) % bands) for i in range(bands)])
                pieces.append(piece)
        else:
            sent = jnp.stack([field[t * band + low : t * band + high] for t in range(bands)])
            got = lax.all_to_all(sent, "filt", split_axis=0, concat_axis=0, tiled=True)
            pieces.append(jnp.transpose(got, (1, 2, 0, 3, 4)).reshape(high - low, planes, C, width))
        travelled.append(pieces)

    if count % 16 == 0:
        order = lax.rem(me - jnp.arange(bands, dtype=jnp.int32) + bands, bands)
    else:
        order = jnp.zeros((1,), jnp.int32)
    order, first, second = lax.optimization_barrier((order, first, second))

    blocks, outs, done_rows = [], [], 0
    for (low, high), pieces in zip(chunks, travelled):
        own = pl.pallas_call(
            gather_kernel,
            out_shape=jax.ShapeDtypeStruct((high - low, planes, C, width), jnp.bfloat16),
            in_specs=[smem] + [vmem] * len(pieces),
            out_specs=vmem,
            compiler_params=params,
        )(order, *pieces)
        blocks.append((low, high, (shifted(own, "space", 1), own, shifted(own[:, :1], "space", -1))))
        last = (high - 3) // 2
        used = [block for block in blocks if block[1] > 2 * done_rows]
        rows = []
        for r in range(2 * done_rows, 2 * last + 3):
            rows += [(i, r - block[0]) for i, block in enumerate(used) if block[0] <= r < block[1]]
        top = (me > 0).astype(jnp.int32) if done_rows == 0 else jnp.ones((), jnp.int32)
        edge = jnp.stack([space.astype(jnp.int32), top])
        operands = [array for block in used for array in block[2]]
        outs.append(
            pl.pallas_call(
                functools.partial(conv_kernel, rows),
                out_shape=jax.ShapeDtypeStruct((last - done_rows, C2, width // 2), jnp.bfloat16),
                in_specs=[smem] + [vmem] * (2 + len(operands)),
                out_specs=vmem,
                scratch_shapes=[
                    pltpu.VMEM((5, len(rows) * 4 * C, width // 2), jnp.bfloat16),
                    pltpu.VMEM(((len(rows) - 2) * 9 * C, width // 2), jnp.bfloat16),
                ],
                compiler_params=params,
            )(edge, first, second, *operands)
        )
        done_rows = last
    coarse = jnp.concatenate(outs)
    return jnp.transpose(coarse, (1, 0, 2))[:, None]


def solution(mesh):
    return jax.shard_map(
        local,
        mesh=mesh,
        in_specs=(P("filt", ("groups", "space"), None, None), P(), P()),
        out_specs=P(None, ("groups", "space"), "filt", None),
        check_vma=False,
    )
```

```python
import functools

import jax
import jax.numpy as jnp
from jax import lax
from jax.experimental import pallas as pl
from jax.experimental.pallas import tpu as pltpu
from jax.sharding import PartitionSpec as P

C = 64
C2 = 128
BELOW, ABOVE = 2, 1
negative_slope = 0.01
VMEM_LIMIT = 56 * 1024 * 1024


def split_matrix(width):
    half = width // 2
    source = lax.broadcasted_iota(jnp.int32, (width, width), 0)
    column = lax.broadcasted_iota(jnp.int32, (width, width), 1)
    wanted = jnp.where(column < half, 2 * column, 2 * (column - half) + 1)
    return jnp.where(source == wanted, 1.0, 0.0).astype(jnp.bfloat16)


def turn_matrix(count, rows):
    size = count * rows
    target = lax.broadcasted_iota(jnp.int32, (size, size), 0)
    source = lax.broadcasted_iota(jnp.int32, (size, size), 1)
    wanted = lax.rem(target, count) * rows + lax.div(target, count)
    return jnp.where(source == wanted, 1.0, 0.0).astype(jnp.bfloat16)


def send_kernel(band, parts, start_ref, volume_ref, *refs):
    out_refs, field_ref = refs[:-1], refs[-1]
    count, planes, all_rows, width = volume_ref.shape
    step = 16
    split, turn = split_matrix(width), turn_matrix(count, step)
    field_ref[pl.ds(0, BELOW)] = jnp.zeros((BELOW, planes, count, width), jnp.bfloat16)
    field_ref[pl.ds(BELOW + all_rows, ABOVE)] = jnp.zeros((ABOVE, planes, count, width), jnp.bfloat16)
    for p in range(planes):
        for at in range(0, all_rows, step):
            block = volume_ref[:, p, at : at + step, :].reshape(count * step, width)
            block = jnp.dot(block, split, preferred_element_type=jnp.float32).astype(jnp.bfloat16)
            block = jnp.dot(turn, block, preferred_element_type=jnp.float32).astype(jnp.bfloat16)
            field_ref[pl.ds(BELOW + at, step), p] = block.reshape(step, count, width)
    for (which, low, high), out_ref in zip(parts, out_refs):
        out_ref[...] = field_ref[pl.ds(start_ref[which] + low, high - low)]


def conv_kernel(parts, window, edge_ref, order_ref, first_ref, second_ref, *refs):
    blocks, (out_ref, taps_ref, hid_ref) = refs[:-3], refs[-3:]
    half = out_ref.shape[2]
    for i, (which, low, high) in enumerate(parts):
        below_ref, own_ref, above_ref = blocks[3 * i : 3 * i + 3]
        count = own_ref.shape[2]
        lane = lax.broadcasted_iota(jnp.int32, (count, half), 1)
        at = pl.multiple_of(order_ref[which] * count, count)
        for r in range(low, high):
            for p in range(5):
                cell = (below_ref, own_ref, above_ref)[p // 2][r - low, p % 2]
                even, odd = cell[:, :half], cell[:, half:]
                before = jnp.where(lane == 0, 0.0, pltpu.roll(odd.astype(jnp.float32), 1, 1))
                after = jnp.where(lane == half - 1, 0.0, pltpu.roll(even.astype(jnp.float32), half - 1, 1))
                shifts = (before.astype(jnp.bfloat16), even, odd, after.astype(jnp.bfloat16))
                for k, value in enumerate(shifts):
                    taps_ref[p, pl.ds((4 * r + k) * C + at, count), :] = value
    size = 2 * C
    lane = lax.broadcasted_iota(jnp.int32, (C, half), 1)
    for y in range(window - 2):
        total = [None] * 3
        for p in range(5):
            z_low, z_high = max(0, p - 2), min(2, p)
            first = 2 - (p - z_low)
            weight = first_ref[pl.ds(first * size, (z_high - z_low + 1) * size), :]
            part = jnp.dot(
                weight, taps_ref[p, pl.ds(y * 4 * C, 12 * C), :], preferred_element_type=jnp.float32
            )
            for z in range(z_low, z_high + 1):
                piece = part[(z - z_low) * size : (z - z_low + 1) * size]
                total[z] = piece if total[z] is None else total[z] + piece
        for z in range(3):
            value = total[z]
            value = jnp.where(value > 0, value, negative_slope * value)
            if z == 0:
                value = jnp.where(edge_ref[0] > 0, value, 0.0)
            if y == 0:
                value = jnp.where(edge_ref[1] > 0, value, 0.0)
            value = value.astype(jnp.bfloat16)
            before = jnp.where(lane == 0, 0.0, pltpu.roll(value[C:].astype(jnp.float32), 1, 1))
            base = (y * 3 + z) * 3 * C
            hid_ref[pl.ds(base, C), :] = before.astype(jnp.bfloat16)
            hid_ref[pl.ds(base + C, 2 * C), :] = value
    for y in range(out_ref.shape[0]):
        out_ref[y] = jnp.dot(
            second_ref[...], hid_ref[pl.ds(2 * y * 9 * C, 27 * C), :], preferred_element_type=jnp.float32
        ).astype(jnp.bfloat16)


def first_weights(conv_weight):
    shaped = jnp.transpose(conv_weight.reshape(3, 3, 3, C, C), (0, 3, 1, 2, 4))
    shaped = shaped[::-1]
    even = jnp.pad(shaped, ((0, 0), (0, 0), (0, 0), (0, 1), (0, 0)))
    odd = jnp.pad(shaped, ((0, 0), (0, 0), (0, 0), (1, 0), (0, 0)))
    return jnp.stack([even, odd], axis=1).reshape(3 * 2 * C, 12 * C)


def second_weights(down_weight):
    shaped = down_weight.reshape(3, 3, 3, C2, C)
    return jnp.transpose(shaped, (3, 1, 0, 2, 4)).reshape(C2, 27 * C)


def shifted(block, axis, by):
    count = lax.axis_size(axis)
    return lax.ppermute(block, axis, [(i, i + by) for i in range(count) if 0 <= i + by < count])


def after(value, *others):
    return lax.optimization_barrier((value, *others))[0]


def local(volume, conv_weight, down_weight):
    bands = lax.axis_size("filt")
    me = lax.axis_index("filt").astype(jnp.int32)
    space = lax.axis_index("space").astype(jnp.int32)
    count, planes, all_rows, width = volume.shape
    band = all_rows // bands
    window = BELOW + band + ABOVE
    vmem = pl.BlockSpec(memory_space=pltpu.VMEM)
    smem = pl.BlockSpec(memory_space=pltpu.SMEM)
    params = pltpu.CompilerParams(vmem_limit_bytes=VMEM_LIMIT)
    distance = jnp.arange(bands, dtype=jnp.int32)
    own = []
    first, second = first_weights(conv_weight), second_weights(down_weight)
    if count == 16 and bands == 4:
        parts = [(d, 0, window) for d in (0, 3, 1, 2)]
        sent = pl.pallas_call(
            functools.partial(send_kernel, band, parts),
            out_shape=[
                jax.ShapeDtypeStruct((high - low, planes, count, width), jnp.bfloat16)
                for _, low, high in parts
            ],
            in_specs=[smem, vmem],
            out_specs=[vmem] * len(parts),
            scratch_shapes=[
                pltpu.VMEM((BELOW + all_rows + ABOVE, planes, count, width), jnp.bfloat16)
            ],
            compiler_params=params,
        )(lax.rem(me + distance, bands) * band, volume)
        for (d, _, _), piece in zip(parts, sent):
            if d:
                piece = lax.ppermute(piece, "filt", [(i, (i + d) % bands) for i in range(bands)])
            own.append(piece)
        order = lax.rem(me - distance + bands, bands)
        own[0], own[1], first, second, order = lax.optimization_barrier((own[0], own[1], first, second, order))
    else:
        parts = [(0, 0, window)]
        field = jnp.transpose(volume, (2, 1, 0, 3))
        field = jnp.concatenate([field[..., ::2], field[..., 1::2]], axis=-1)
        field = jnp.pad(field, ((BELOW, ABOVE), (0, 0), (0, 0), (0, 0)))
        sent = jnp.stack([field[t * band : t * band + window] for t in range(bands)])
        got = lax.all_to_all(sent, "filt", split_axis=0, concat_axis=0, tiled=True)
        own.append(jnp.transpose(got, (1, 2, 0, 3, 4)).reshape(window, planes, C, width))
        order = jnp.zeros((1,), jnp.int32)
    triples = []
    for i, piece in enumerate(own):
        if i > 1:
            piece = after(piece, *triples[i - 2])
        triples.append((shifted(piece, "space", 1), piece, shifted(piece, "space", -1)))
    operands = [array for triple in triples for array in triple]
    coarse = pl.pallas_call(
        functools.partial(conv_kernel, parts, window),
        out_shape=jax.ShapeDtypeStruct((band // 2, C2, width // 2), jnp.bfloat16),
        in_specs=[smem] * 2 + [vmem] * (2 + len(operands)),
        out_specs=vmem,
        scratch_shapes=[
            pltpu.VMEM((5, window * 4 * C, width // 2), jnp.bfloat16),
            pltpu.VMEM(((band + 1) * 9 * C, width // 2), jnp.bfloat16),
        ],
        compiler_params=params,
    )(jnp.stack([space, me]), order, first, second, *operands)
    return jnp.transpose(coarse, (1, 0, 2))[:, None]


def solution(mesh):
    return jax.shard_map(
        local,
        mesh=mesh,
        in_specs=(P("filt", ("groups", "space"), None, None), P(), P()),
        out_specs=P(None, ("groups", "space"), "filt", None),
        check_vma=False,
    )
```

```python
import functools

import jax
import jax.numpy as jnp
from jax import lax
from jax.experimental import pallas as pl
from jax.experimental.pallas import tpu as pltpu
from jax.sharding import PartitionSpec as P

C = 64
C2 = 128
BELOW, ABOVE = 2, 1
negative_slope = 0.01
VMEM_LIMIT = 20 * 1024 * 1024


def split_matrix(width):
    half = width // 2
    source = lax.broadcasted_iota(jnp.int32, (width, width), 0)
    column = lax.broadcasted_iota(jnp.int32, (width, width), 1)
    wanted = jnp.where(column < half, 2 * column, 2 * (column - half) + 1)
    return jnp.where(source == wanted, 1.0, 0.0).astype(jnp.bfloat16)


def turn_matrix(count, rows):
    size = count * rows
    target = lax.broadcasted_iota(jnp.int32, (size, size), 0)
    source = lax.broadcasted_iota(jnp.int32, (size, size), 1)
    wanted = lax.rem(target, count) * rows + lax.div(target, count)
    return jnp.where(source == wanted, 1.0, 0.0).astype(jnp.bfloat16)


def send_kernel(band, distances, volume_ref, *refs):
    out_refs, field_ref = refs[:-1], refs[-1]
    count, planes, all_rows, width = volume_ref.shape
    step = 16
    split, turn = split_matrix(width), turn_matrix(count, step)
    field_ref[pl.ds(0, BELOW)] = jnp.zeros((BELOW, planes, count, width), jnp.bfloat16)
    field_ref[pl.ds(BELOW + all_rows, ABOVE)] = jnp.zeros((ABOVE, planes, count, width), jnp.bfloat16)
    for p in range(planes):
        for at in range(0, all_rows, step):
            block = volume_ref[:, p, at : at + step, :].reshape(count * step, width)
            block = jnp.dot(block, split, preferred_element_type=jnp.float32).astype(jnp.bfloat16)
            block = jnp.dot(turn, block, preferred_element_type=jnp.float32).astype(jnp.bfloat16)
            field_ref[pl.ds(BELOW + at, step), p] = block.reshape(step, count, width)
    me, bands = lax.axis_index("filt"), lax.axis_size("filt")
    for d, out_ref in zip(distances, out_refs):
        start = lax.rem(me + d, bands) * band
        out_ref[...] = field_ref[pl.ds(start, out_ref.shape[0])]


def store_taps(taps_ref, row, at, channels, cell):
    count, half = cell.shape[0], cell.shape[1] // 2
    lane = lax.broadcasted_iota(jnp.int32, (count, half), 1)
    even, odd = cell[:, :half], cell[:, half:]
    before = jnp.where(lane == 0, 0.0, pltpu.roll(odd.astype(jnp.float32), 1, 1))
    after_it = jnp.where(lane == half - 1, 0.0, pltpu.roll(even.astype(jnp.float32), half - 1, 1))
    for k, value in enumerate((before.astype(jnp.bfloat16), even, odd, after_it.astype(jnp.bfloat16))):
        taps_ref[pl.ds((4 * row + k) * channels + at, count), :] = value


def plane_parts(total, weight_ref, taps, y, p, depth):
    size = 2 * C
    z_low, z_high = max(0, p - 2), min(2, p)
    first = 2 - (p - z_low)
    weight = weight_ref[pl.ds(first * size, (z_high - z_low + 1) * size), :]
    part = jnp.dot(weight, taps[pl.ds(y * depth, 3 * depth), :], preferred_element_type=jnp.float32)
    for z in range(z_low, z_high + 1):
        piece = part[(z - z_low) * size : (z - z_low + 1) * size]
        total[z] = piece if total[z] is None else total[z] + piece


def early_kernel(parts, late, window, first_ref, *refs):
    blocks, (out_ref, taps_ref) = refs[:-2], refs[-2:]
    half = out_ref.shape[1]
    for i, row, at, planes in parts:
        for r in range(window):
            for k, p in enumerate(planes):
                if p is not None:
                    store_taps(taps_ref.at[p], r, at, C, blocks[i][row + r, k])
    if late:
        empty = jnp.zeros((late, half), jnp.bfloat16)
        for p in (0, 1, 4):
            for r in range(4 * window):
                taps_ref[p, pl.ds(r * C + C - late, late), :] = empty
    for y in range(window - 2):
        total = [None] * 3
        for p in range(5):
            plane_parts(total, first_ref, taps_ref.at[p], y, p, 4 * C)
        for z in range(3):
            out_ref[pl.ds((y * 3 + z) * 2 * C, 2 * C), :] = total[z]


def late_kernel(late, window, edge_ref, feature_ref, second_ref, *refs):
    out_ref, hid_ref = refs[-2:] if not late else refs[-3:-1]
    half = out_ref.shape[2]
    if late:
        weight_ref, below_ref, above_ref, taps_ref = refs[0], refs[1], refs[2], refs[-1]
        for r in range(window):
            store_taps(taps_ref.at[0], r, 0, late, below_ref[r, 0])
            store_taps(taps_ref.at[1], r, 0, late, below_ref[r, 1])
            store_taps(taps_ref.at[2], r, 0, late, above_ref[r, 0])
    size = 2 * C
    lane = lax.broadcasted_iota(jnp.int32, (C, half), 1)
    for y in range(window - 2):
        total = [feature_ref[pl.ds((y * 3 + z) * size, size), :] for z in range(3)]
        if late:
            for k, p in enumerate((0, 1, 4)):
                plane_parts(total, weight_ref, taps_ref.at[k], y, p, 4 * late)
        for z in range(3):
            value = total[z]
            value = jnp.where(value > 0, value, negative_slope * value)
            if z == 0:
                value = jnp.where(edge_ref[0] > 0, value, 0.0)
            if y == 0:
                value = jnp.where(edge_ref[1] > 0, value, 0.0)
            value = value.astype(jnp.bfloat16)
            before = jnp.where(lane == 0, 0.0, pltpu.roll(value[C:].astype(jnp.float32), 1, 1))
            base = (y * 3 + z) * 3 * C
            hid_ref[pl.ds(base, C), :] = before.astype(jnp.bfloat16)
            hid_ref[pl.ds(base + C, 2 * C), :] = value
    for y in range(out_ref.shape[0]):
        out_ref[y] = jnp.dot(
            second_ref[...], hid_ref[pl.ds(2 * y * 9 * C, 27 * C), :], preferred_element_type=jnp.float32
        ).astype(jnp.bfloat16)


def first_weights(conv_weight, turn):
    shaped = conv_weight.reshape(3, 3, 3, C, C)
    if turn is not None:
        shaped = jnp.dot(shaped, turn, preferred_element_type=jnp.float32).astype(jnp.bfloat16)
    shaped = jnp.transpose(shaped, (0, 3, 1, 2, 4))[::-1]
    even = jnp.pad(shaped, ((0, 0), (0, 0), (0, 0), (0, 1), (0, 0)))
    odd = jnp.pad(shaped, ((0, 0), (0, 0), (0, 0), (1, 0), (0, 0)))
    return jnp.stack([even, odd], axis=1).reshape(3 * 2 * C, 12 * C)


def second_weights(down_weight):
    shaped = down_weight.reshape(3, 3, 3, C2, C)
    return jnp.transpose(shaped, (3, 1, 0, 2, 4)).reshape(C2, 27 * C)


def shifted(block, axis, by):
    count = lax.axis_size(axis)
    return lax.ppermute(block, axis, [(i, i + by) for i in range(count) if 0 <= i + by < count])


def after(value, *others):
    return lax.optimization_barrier((value, *others))[0]


def in_vmem(value):
    return pltpu.with_memory_space_constraint(value, pltpu.VMEM)


def block_order(me, distances, bands, count):
    row = lax.broadcasted_iota(jnp.int32, (C, C), 0)
    column = lax.broadcasted_iota(jnp.int32, (C, C), 1)
    piece = column // count
    source = sum(jnp.where(piece == i, lax.rem(me - d + bands, bands), 0) for i, d in enumerate(distances))
    return (row == source * count + column % count).astype(jnp.bfloat16)


def local(volume, conv_weight, down_weight):
    bands = lax.axis_size("filt")
    me = lax.axis_index("filt").astype(jnp.int32)
    space = lax.axis_index("space").astype(jnp.int32)
    count, planes, all_rows, width = volume.shape
    band = all_rows // bands
    window = BELOW + band + ABOVE
    half = width // 2
    vmem = pl.BlockSpec(memory_space=pltpu.VMEM)
    smem = pl.BlockSpec(memory_space=pltpu.SMEM)
    params = pltpu.CompilerParams(vmem_limit_bytes=VMEM_LIMIT)
    second = second_weights(down_weight)
    below, inside, above = (0, 1), (2, 3), (4, None)
    if count == 16 and bands == 4:
        distances = (0, 3, 1, 2)
        sent = pl.pallas_call(
            functools.partial(send_kernel, band, distances),
            out_shape=[pltpu.VMEM((window, planes, count, width), jnp.bfloat16)] * bands,
            in_specs=[vmem],
            out_specs=[vmem] * bands,
            scratch_shapes=[
                pltpu.VMEM((BELOW + all_rows + ABOVE, planes, count, width), jnp.bfloat16)
            ],
            compiler_params=params,
        )(volume)
        own = [
            lax.ppermute(piece, "filt", [(i, (i + d) % bands) for i in range(bands)]) if d else piece
            for d, piece in zip(distances, sent)
        ]
        first = first_weights(conv_weight, block_order(me, distances, bands, count))
        late = count
        last = first.reshape(6 * C, 12, C)[:, :, C - late :].reshape(6 * C, 12 * late)
        mine = after(own[0], own[1])
        middle = jnp.concatenate(own[1:3])
        middle = after(middle, own[1])
        blocks = [own[0], shifted(mine, "space", 1), shifted(mine, "space", -1)]
        blocks += [middle, shifted(middle, "space", 1), shifted(middle, "space", -1), own[3]]
        parts = []
        for i, held in enumerate((inside, below, above)):
            parts += [(i, 0, 0, held), (3 + i, 0, count, held), (3 + i, window, 2 * count, held)]
        parts.append((6, 0, 3 * count, inside))
        tail, first, second, last = lax.optimization_barrier((own[3], first, second, last, *blocks[1:3]))[:4]
        tails = [last, shifted(tail, "space", 1), shifted(tail, "space", -1)]
    else:
        field = jnp.transpose(volume, (2, 1, 0, 3))
        field = jnp.concatenate([field[..., ::2], field[..., 1::2]], axis=-1)
        field = jnp.pad(field, ((BELOW, ABOVE), (0, 0), (0, 0), (0, 0)))
        sent = jnp.stack([field[t * band : t * band + window] for t in range(bands)])
        got = lax.all_to_all(sent, "filt", split_axis=0, concat_axis=0, tiled=True)
        own = jnp.transpose(got, (1, 2, 0, 3, 4)).reshape(window, planes, C, width)
        first = first_weights(conv_weight, None)
        blocks = [own, shifted(own, "space", 1), shifted(own, "space", -1)]
        parts = [(i, 0, 0, held) for i, held in enumerate((inside, below, above))]
        late, tails = 0, []
    hid_rows = band + 1
    feature = pl.pallas_call(
        functools.partial(early_kernel, parts, late, window),
        out_shape=pltpu.VMEM((hid_rows * 6 * C, half), jnp.float32),
        in_specs=[vmem] * (1 + len(blocks)),
        out_specs=vmem,
        scratch_shapes=[pltpu.VMEM((5, window * 4 * C, half), jnp.bfloat16)],
        compiler_params=params,
    )(in_vmem(first), *map(in_vmem, blocks))
    coarse = pl.pallas_call(
        functools.partial(late_kernel, late, window),
        out_shape=pltpu.VMEM((band // 2, C2, half), jnp.bfloat16),
        in_specs=[smem] + [vmem] * (2 + len(tails)),
        out_specs=vmem,
        scratch_shapes=[pltpu.VMEM((hid_rows * 9 * C, half), jnp.bfloat16)]
        + [pltpu.VMEM((3, window * 4 * late, half), jnp.bfloat16)] * (late > 0),
        compiler_params=params,
    )(jnp.stack([space, me]), in_vmem(feature), in_vmem(second), *map(in_vmem, tails))
    return jnp.transpose(coarse, (1, 0, 2))[:, None]


def solution(mesh):
    return jax.shard_map(
        local,
        mesh=mesh,
        in_specs=(P("filt", ("groups", "space"), None, None), P(), P()),
        out_specs=P(None, ("groups", "space"), "filt", None),
        check_vma=False,
    )
```

```python
import functools

import jax
import jax.numpy as jnp
from jax import lax
from jax.experimental import pallas as pl
from jax.experimental.pallas import tpu as pltpu
from jax.sharding import PartitionSpec as P

C = 64
C2 = 128
BELOW, ABOVE = 2, 1
negative_slope = 0.01
VMEM_LIMIT = 20 * 1024 * 1024


def split_matrix(width):
    half = width // 2
    source = lax.broadcasted_iota(jnp.int32, (width, width), 0)
    column = lax.broadcasted_iota(jnp.int32, (width, width), 1)
    wanted = jnp.where(column < half, 2 * column, 2 * (column - half) + 1)
    return jnp.where(source == wanted, 1.0, 0.0).astype(jnp.bfloat16)


def turn_matrix(count, rows):
    size = count * rows
    target = lax.broadcasted_iota(jnp.int32, (size, size), 0)
    source = lax.broadcasted_iota(jnp.int32, (size, size), 1)
    wanted = lax.rem(target, count) * rows + lax.div(target, count)
    return jnp.where(source == wanted, 1.0, 0.0).astype(jnp.bfloat16)


def send_kernel(band, distances, volume_ref, *refs):
    out_refs, field_ref = refs[:-1], refs[-1]
    count, planes, all_rows, width = volume_ref.shape
    step = 16
    split, turn = split_matrix(width), turn_matrix(count, step)
    field_ref[pl.ds(0, BELOW)] = jnp.zeros((BELOW, planes, count, width), jnp.bfloat16)
    field_ref[pl.ds(BELOW + all_rows, ABOVE)] = jnp.zeros((ABOVE, planes, count, width), jnp.bfloat16)
    for p in range(planes):
        for at in range(0, all_rows, step):
            block = volume_ref[:, p, at : at + step, :].reshape(count * step, width)
            block = jnp.dot(block, split, preferred_element_type=jnp.float32).astype(jnp.bfloat16)
            block = jnp.dot(turn, block, preferred_element_type=jnp.float32).astype(jnp.bfloat16)
            field_ref[pl.ds(BELOW + at, step), p] = block.reshape(step, count, width)
    me, bands = lax.axis_index("filt"), lax.axis_size("filt")
    for d, out_ref in zip(distances, out_refs):
        start = lax.rem(me + d, bands) * band
        out_ref[...] = field_ref[pl.ds(start, out_ref.shape[0])]


def store_taps(taps_ref, row, at, channels, cell):
    count, half = cell.shape[0], cell.shape[1] // 2
    lane = lax.broadcasted_iota(jnp.int32, (count, half), 1)
    even, odd = cell[:, :half], cell[:, half:]
    before = jnp.where(lane == 0, 0.0, pltpu.roll(odd.astype(jnp.float32), 1, 1))
    after_it = jnp.where(lane == half - 1, 0.0, pltpu.roll(even.astype(jnp.float32), half - 1, 1))
    for k, value in enumerate((before.astype(jnp.bfloat16), even, odd, after_it.astype(jnp.bfloat16))):
        taps_ref[pl.ds((4 * row + k) * channels + at, count), :] = value


def plane_parts(total, weight_ref, taps, y, p, depth):
    size = 2 * C
    z_low, z_high = max(0, p - 2), min(2, p)
    first = 2 - (p - z_low)
    weight = weight_ref[pl.ds(first * size, (z_high - z_low + 1) * size), :]
    part = jnp.dot(weight, taps[pl.ds(y * depth, 3 * depth), :], preferred_element_type=jnp.float32)
    for z in range(z_low, z_high + 1):
        piece = part[(z - z_low) * size : (z - z_low + 1) * size]
        total[z] = piece if total[z] is None else total[z] + piece


def early_kernel(parts, late, window, places_ref, first_ref, *refs):
    blocks, (out_ref, taps_ref) = refs[:-2], refs[-2:]
    half = out_ref.shape[1]
    for i, row, at, held in parts:
        for r in range(window):
            for k in range(2):
                store_taps(taps_ref.at[places_ref[2 * held + k]], r, at, C, blocks[i][row + r, k])
    if late:
        empty = jnp.zeros((late, half), jnp.bfloat16)
        for p in (0, 1, 4):
            for r in range(4 * window):
                taps_ref[p, pl.ds(r * C + C - late, late), :] = empty
    for y in range(window - 2):
        total = [None] * 3
        for p in range(5):
            plane_parts(total, first_ref, taps_ref.at[p], y, p, 4 * C)
        for z in range(3):
            out_ref[pl.ds((y * 3 + z) * 2 * C, 2 * C), :] = total[z]


def late_kernel(late, window, edge_ref, feature_ref, second_ref, *refs):
    out_ref, hid_ref = refs[-2:] if not late else refs[-3:-1]
    half = out_ref.shape[2]
    if late:
        weight_ref, taps_ref = refs[0], refs[-1]
        for i in range(2):
            for r in range(window):
                for k in range(2):
                    place = edge_ref[2 + 2 * i + k]
                    store_taps(taps_ref.at[place], r, 0, late, refs[1 + i][r, k])
    size = 2 * C
    lane = lax.broadcasted_iota(jnp.int32, (C, half), 1)
    for y in range(window - 2):
        total = [feature_ref[pl.ds((y * 3 + z) * size, size), :] for z in range(3)]
        if late:
            for k, p in enumerate((0, 1, 4)):
                plane_parts(total, weight_ref, taps_ref.at[k], y, p, 4 * late)
        for z in range(3):
            value = total[z]
            value = jnp.where(value > 0, value, negative_slope * value)
            if z == 0:
                value = jnp.where(edge_ref[0] > 0, value, 0.0)
            if y == 0:
                value = jnp.where(edge_ref[1] > 0, value, 0.0)
            value = value.astype(jnp.bfloat16)
            before = jnp.where(lane == 0, 0.0, pltpu.roll(value[C:].astype(jnp.float32), 1, 1))
            base = (y * 3 + z) * 3 * C
            hid_ref[pl.ds(base, C), :] = before.astype(jnp.bfloat16)
            hid_ref[pl.ds(base + C, 2 * C), :] = value
    for y in range(out_ref.shape[0]):
        out_ref[y] = jnp.dot(
            second_ref[:, : 27 * C], hid_ref[pl.ds(2 * y * 9 * C, 27 * C), :], preferred_element_type=jnp.float32
        ).astype(jnp.bfloat16)


def exact(left, right):
    return jnp.dot(left, right, preferred_element_type=jnp.float32)


def weight_kernel(distances, conv_ref, down_ref, first_ref, second_ref, *refs):
    row = lax.broadcasted_iota(jnp.int32, (C, 2 * C), 0)
    lane = lax.broadcasted_iota(jnp.int32, (C, 2 * C), 1)
    low, high = (row == lane).astype(jnp.bfloat16), (row == lane - C).astype(jnp.bfloat16)
    for j in range(14):
        total = None
        for t, place in ((2 * j, low), (2 * j + 1, high)):
            if t < 27:
                tap = down_ref[t // 3 % 3 * 9 + t // 9 * 3 + t % 3]
                part = exact(tap, place)
                total = part if total is None else total + part
        second_ref[:, pl.ds(2 * C * j, 2 * C)] = total.astype(jnp.bfloat16)
    if distances:
        me, bands = lax.axis_index("filt"), len(distances)
        count = C // bands
        block, inside = lane % C // count, lane % count
        source = jnp.zeros_like(lane)
        for i, d in enumerate(distances):
            source = jnp.where(block == i, lax.rem(me - d + bands, bands), source)
        wanted = row == source * count + inside
        low, high = [(wanted & (lane // C == k)).astype(jnp.bfloat16) for k in range(2)]
    for a in range(3):
        taps = [jnp.concatenate([conv_ref[9 * a + 3 * b + c] for b in range(3)]) for c in range(3)]
        lows, highs = [[exact(tap, place) for tap in taps] for place in (low, high)]
        tiles = ((lows[0] + highs[1], lows[2]), (highs[0], lows[1] + highs[2]))
        for parity in range(2):
            for k in range(2):
                tile = tiles[parity][k].astype(jnp.bfloat16)
                for b in range(3):
                    at = (2 - a) * 2 * C + parity * C
                    first_ref[pl.ds(at, C), pl.ds((2 * b + k) * 2 * C, 2 * C)] = tile[b * C : (b + 1) * C]
    if distances:
        last_ref = refs[0]
        row = lax.broadcasted_iota(jnp.int32, (C, 12 * count), 0)
        lane = lax.broadcasted_iota(jnp.int32, (C, 12 * count), 1)
        source = lax.rem(me - distances[-1] + bands, bands) * count
        for parity in range(2):
            total = None
            for b in range(3):
                for c in range(3):
                    taps = jnp.concatenate([conv_ref[9 * a + 3 * b + c] for a in range(3)])
                    at = (4 * b + c + parity) * count
                    place = (lane >= at) & (lane < at + count) & (row == source + lane - at)
                    part = exact(taps, place.astype(jnp.bfloat16))
                    total = part if total is None else total + part
            total = total.astype(jnp.bfloat16)
            for a in range(3):
                last_ref[pl.ds((2 - a) * 2 * C + parity * C, C), :] = total[a * C : (a + 1) * C]


def swapped(block, axis):
    count = lax.axis_size(axis)
    results = []
    for start in (0, 1):
        pairs = [(i, i + 1) for i in range(start, count - 1, 2)]
        results.append(lax.ppermute(block, axis, pairs + [(j, i) for i, j in pairs]))
    return results


def after(value, *others):
    return lax.optimization_barrier((value, *others))[0]


def in_vmem(value):
    return pltpu.with_memory_space_constraint(value, pltpu.VMEM)


def local(volume, conv_weight, down_weight):
    bands = lax.axis_size("filt")
    me = lax.axis_index("filt").astype(jnp.int32)
    space = lax.axis_index("space").astype(jnp.int32)
    count, planes, all_rows, width = volume.shape
    band = all_rows // bands
    window = BELOW + band + ABOVE
    half = width // 2
    hid_rows = band + 1
    vmem = pl.BlockSpec(memory_space=pltpu.VMEM)
    smem = pl.BlockSpec(memory_space=pltpu.SMEM)
    params = pltpu.CompilerParams(vmem_limit_bytes=VMEM_LIMIT)
    direct = count == 16 and bands == 4
    distances = (0, 3, 1, 2) if direct else ()
    late = count if direct else 0
    lay = pl.pallas_call(
        functools.partial(weight_kernel, distances),
        out_shape=[
            pltpu.VMEM((6 * C, 12 * C), jnp.bfloat16),
            pltpu.VMEM((C2, 28 * C), jnp.bfloat16),
        ]
        + [pltpu.VMEM((6 * C, 12 * late), jnp.bfloat16)] * direct,
        in_specs=[vmem] * 2,
        out_specs=[vmem] * (3 if direct else 2),
        compiler_params=params,
    )
    first, second, *last = lay(conv_weight.reshape(27, C, C), down_weight.reshape(27, C2, C))
    if direct:
        sent = pl.pallas_call(
            functools.partial(send_kernel, band, distances),
            out_shape=[pltpu.VMEM((window, planes, count, width), jnp.bfloat16)] * bands,
            in_specs=[vmem],
            out_specs=[vmem] * bands,
            scratch_shapes=[
                pltpu.VMEM((BELOW + all_rows + ABOVE, planes, count, width), jnp.bfloat16)
            ],
            compiler_params=params,
        )(volume)
        own = []
        for d, piece in zip(distances, sent):
            if d == 2:
                piece = after(piece, own[1])
            if d:
                piece = lax.ppermute(piece, "filt", [(i, (i + d) % bands) for i in range(bands)])
            own.append(piece)
        mine = swapped(after(own[0], first), "space")
        middle = jnp.concatenate(own[1:3])
        middles = swapped(middle, "space")
        tails = last + swapped(after(own[3], *mine), "space")
        blocks = [own[0], *mine, middle, *middles, own[3]]
        parts = []
        for held in range(3):
            parts += [(held, 0, 0, held), (3 + held, 0, count, held), (3 + held, window, 2 * count, held)]
        parts.append((6, 0, 3 * count, 0))
    else:
        field = jnp.transpose(volume, (2, 1, 0, 3))
        field = jnp.concatenate([field[..., ::2], field[..., 1::2]], axis=-1)
        field = jnp.pad(field, ((BELOW, ABOVE), (0, 0), (0, 0), (0, 0)))
        sent = jnp.stack([field[t * band : t * band + window] for t in range(bands)])
        got = lax.all_to_all(sent, "filt", split_axis=0, concat_axis=0, tiled=True)
        own = jnp.transpose(got, (1, 2, 0, 3, 4)).reshape(window, planes, C, width)
        blocks = [own, *swapped(own, "space")]
        parts = [(held, 0, 0, held) for held in range(3)]
        tails = []
    even = space % 2 == 0
    places = [jnp.where(even, p, q) for p, q in ((4, 0), (5, 1), (0, 4), (1, 5))]
    slots = [jnp.where(even, p, q) for p, q in ((2, 0), (3, 1), (0, 2), (1, 3))]
    feature = pl.pallas_call(
        functools.partial(early_kernel, parts, late, window),
        out_shape=pltpu.VMEM((hid_rows * 6 * C, half), jnp.float32),
        in_specs=[smem] + [vmem] * (1 + len(blocks)),
        out_specs=vmem,
        scratch_shapes=[pltpu.VMEM((6, window * 4 * C, half), jnp.bfloat16)],
        compiler_params=params,
    )(jnp.stack([2, 3, *places]).astype(jnp.int32), in_vmem(first), *map(in_vmem, blocks))
    coarse = pl.pallas_call(
        functools.partial(late_kernel, late, window),
        out_shape=pltpu.VMEM((band // 2, C2, half), jnp.bfloat16),
        in_specs=[smem] + [vmem] * (2 + len(tails)),
        out_specs=vmem,
        scratch_shapes=[pltpu.VMEM((hid_rows * 9 * C, half), jnp.bfloat16)]
        + [pltpu.VMEM((4, window * 4 * late, half), jnp.bfloat16)] * direct,
        compiler_params=params,
    )(
        jnp.stack([space, me, *slots]).astype(jnp.int32),
        in_vmem(feature),
        in_vmem(second),
        *map(in_vmem, tails),
    )
    return jnp.transpose(coarse, (1, 0, 2))[:, None]


def solution(mesh):
    return jax.shard_map(
        local,
        mesh=mesh,
        in_specs=(P("filt", ("groups", "space"), None, None), P(), P()),
        out_specs=P(None, ("groups", "space"), "filt", None),
        check_vma=False,
    )
```

```python
import functools

import jax
import jax.numpy as jnp
from jax import lax
from jax.experimental import pallas as pl
from jax.experimental.pallas import tpu as pltpu
from jax.sharding import PartitionSpec as P

C = 64
C2 = 128
BELOW, ABOVE = 2, 1
negative_slope = 0.01
VMEM_LIMIT = 20 * 1024 * 1024


def split_matrix(width):
    half = width // 2
    source = lax.broadcasted_iota(jnp.int32, (width, width), 0)
    column = lax.broadcasted_iota(jnp.int32, (width, width), 1)
    wanted = jnp.where(column < half, 2 * column, 2 * (column - half) + 1)
    return jnp.where(source == wanted, 1.0, 0.0).astype(jnp.bfloat16)


def turn_matrix(count, rows):
    size = count * rows
    target = lax.broadcasted_iota(jnp.int32, (size, size), 0)
    source = lax.broadcasted_iota(jnp.int32, (size, size), 1)
    wanted = lax.rem(target, count) * rows + lax.div(target, count)
    return jnp.where(source == wanted, 1.0, 0.0).astype(jnp.bfloat16)


def send_kernel(band, distances, volume_ref, *refs):
    out_refs, (block_ref, field_ref, sems) = refs[:-3], refs[-3:]
    count, planes, all_rows, width = volume_ref.shape
    step = block_ref.shape[2]
    places = [(p, at) for at in range(0, all_rows, step) for p in range(planes)]
    copies = [
        pltpu.make_async_copy(volume_ref.at[:, p, pl.ds(at, step), :], block_ref.at[i], sems.at[i])
        for i, (p, at) in enumerate(places)
    ]
    for copy in copies:
        copy.start()
    split, turn = split_matrix(width), turn_matrix(count, step)
    field_ref[pl.ds(0, BELOW)] = jnp.zeros((BELOW, planes, count, width), jnp.bfloat16)
    field_ref[pl.ds(BELOW + all_rows, ABOVE)] = jnp.zeros((ABOVE, planes, count, width), jnp.bfloat16)
    for i, (p, at) in enumerate(places):
        copies[i].wait()
        block = block_ref[i].reshape(count * step, width)
        block = jnp.dot(block, split, preferred_element_type=jnp.float32).astype(jnp.bfloat16)
        block = jnp.dot(turn, block, preferred_element_type=jnp.float32).astype(jnp.bfloat16)
        field_ref[pl.ds(BELOW + at, step), p] = block.reshape(step, count, width)
    me = lax.axis_index("filt")
    for d, out_ref in zip(distances, out_refs):
        start = lax.bitwise_xor(me, d) * band
        out_ref[...] = field_ref[pl.ds(start, out_ref.shape[0])]


def store_taps(taps_ref, row, at, channels, cell):
    count, half = cell.shape[0], cell.shape[1] // 2
    lane = lax.broadcasted_iota(jnp.int32, (count, half), 1)
    even, odd = cell[:, :half], cell[:, half:]
    before = jnp.where(lane == 0, 0.0, pltpu.roll(odd.astype(jnp.float32), 1, 1))
    after_it = jnp.where(lane == half - 1, 0.0, pltpu.roll(even.astype(jnp.float32), half - 1, 1))
    for k, value in enumerate((before.astype(jnp.bfloat16), even, odd, after_it.astype(jnp.bfloat16))):
        taps_ref[pl.ds((4 * row + k) * channels + at, count), :] = value


def plane_parts(total, weight_ref, taps, y, p, depth):
    size = 2 * C
    z_low, z_high = max(0, p - 2), min(2, p)
    first = 2 - (p - z_low)
    weight = weight_ref[pl.ds(first * size, (z_high - z_low + 1) * size), :]
    part = jnp.dot(weight, taps[pl.ds(y * depth, 3 * depth), :], preferred_element_type=jnp.float32)
    for z in range(z_low, z_high + 1):
        piece = part[(z - z_low) * size : (z - z_low + 1) * size]
        total[z] = piece if total[z] is None else total[z] + piece


def join_kernel(one_ref, two_ref, out_ref):
    rows = one_ref.shape[0]
    out_ref[:rows] = one_ref[...]
    out_ref[rows:] = two_ref[...]


class Group:
    def __init__(self, inside, channels, blocks):
        self.inside, self.channels, self.blocks = inside, channels, blocks
        self.planes = (2, 3) if inside else (0, 1, 4)
        self.arrays = 1 + max(i for i, _, _ in blocks)


def conv_kernel(groups, window, first, last, *refs):
    space, band = lax.axis_index("space"), lax.axis_index("filt")
    odd = lax.rem(space, 2)
    places = ((2 - 2 * odd, 3 - 2 * odd), (2 * odd, 1 + 2 * odd))
    refs = list(refs)
    feature_ref = None if first else refs.pop(0)
    second_ref = refs.pop(0) if last else None
    inputs = [[refs.pop(0) for _ in range(1 + group.arrays)] for group in groups]
    out_ref = refs.pop(0)
    hid_ref = refs.pop(0) if last else None
    half = out_ref.shape[-1]
    for group, (_, *blocks), taps_ref in zip(groups, inputs, refs):
        for i, row, at in group.blocks:
            for r in range(window):
                for k in range(2):
                    place = k if group.inside else places[i % 2][k]
                    store_taps(taps_ref.at[place], r, at, group.channels, blocks[i][row + r, k])
    size = 2 * C
    lane = lax.broadcasted_iota(jnp.int32, (C, half), 1)
    for y in range(window - 2):
        total = [None if first else feature_ref[pl.ds((y * 3 + z) * size, size), :] for z in range(3)]
        for group, (weight_ref, *_), taps_ref in zip(groups, inputs, refs):
            for k, p in enumerate(group.planes):
                plane_parts(total, weight_ref, taps_ref.at[k], y, p, 4 * group.channels)
        for z in range(3):
            if not last:
                out_ref[pl.ds((y * 3 + z) * size, size), :] = total[z]
                continue
            value = total[z]
            value = jnp.where(value > 0, value, negative_slope * value)
            if z == 0:
                value = jnp.where(space > 0, value, 0.0)
            if y == 0:
                value = jnp.where(band > 0, value, 0.0)
            value = value.astype(jnp.bfloat16)
            before = jnp.where(lane == 0, 0.0, pltpu.roll(value[C:].astype(jnp.float32), 1, 1))
            base = (y * 3 + z) * 3 * C
            hid_ref[pl.ds(base, C), :] = before.astype(jnp.bfloat16)
            hid_ref[pl.ds(base + C, 2 * C), :] = value
    if last:
        for y in range(out_ref.shape[0]):
            out_ref[y] = jnp.dot(
                second_ref[:, : 27 * C],
                hid_ref[pl.ds(2 * y * 9 * C, 27 * C), :],
                preferred_element_type=jnp.float32,
            ).astype(jnp.bfloat16)


def exact(left, right):
    return jnp.dot(left, right, preferred_element_type=jnp.float32)


def weight_kernel(distances, ranges, conv_ref, down_ref, second_ref, *first_refs):
    row = lax.broadcasted_iota(jnp.int32, (2 * C, 2 * C), 0)
    lane = lax.broadcasted_iota(jnp.int32, (2 * C, 2 * C), 1)
    hidden = 2 * lax.rem(lane, C // 2) + lax.div(lax.rem(lane, C), C // 2)
    pair = [
        [((row == C * odd + hidden) & (lax.div(lane, C) == k)).astype(jnp.bfloat16) for k in range(2)]
        for odd in range(2)
    ]
    in_order = (row == 2 * lax.rem(lane, C) + lax.div(lane, C)).astype(jnp.bfloat16)
    down = [[down_ref[a, b].reshape(3, C, 2 * C) for b in range(3)] for a in range(3)]
    for j in range(14):
        halves = []
        for odd in range(2):
            total = None
            for k in range(2):
                t = 2 * j + k
                if t < 27:
                    part = exact(down[t // 3 % 3][t // 9][t % 3], pair[odd][k])
                    total = part if total is None else total + part
            halves.append(total.astype(jnp.bfloat16))
        second_ref[:, pl.ds(2 * C * j, 2 * C)] = exact(in_order, jnp.concatenate(halves)).astype(jnp.bfloat16)
    conv = [[conv_ref[a, b].reshape(3, C // 2, 2 * C) for b in range(3)] for a in range(3)]
    taps = [[jnp.concatenate([conv[a][b][c] for a in range(3)]) for c in range(3)] for b in range(3)]
    for (start, channels), first_ref in zip(ranges, first_refs):
        row = lax.broadcasted_iota(jnp.int32, (2 * C, 12 * channels), 0)
        lane = lax.broadcasted_iota(jnp.int32, (2 * C, 12 * channels), 1)
        place = start + lax.rem(lane, channels)
        source = place
        if distances:
            me, count = lax.axis_index("filt"), C // len(distances)
            for i, d in enumerate(distances):
                moved = lax.bitwise_xor(me, d) * count + place - i * count
                source = jnp.where(lax.div(place, count) == i, moved, source)
        for odd in range(2):
            shift = jnp.where(row == C * odd + source, lax.div(lane, channels), -1)
            for parity in range(2):
                total = None
                for b in range(3):
                    for c in range(3):
                        part = exact(taps[b][c], (shift == 4 * b + c + parity).astype(jnp.bfloat16))
                        total = part if total is None else total + part
                total = total.astype(jnp.bfloat16)
                for a in range(3):
                    at = (2 - a) * 2 * C + parity * C + odd * C // 2
                    first_ref[pl.ds(at, C // 2), :] = total[a * C // 2 : (a + 1) * C // 2]


def swapped(block, axis):
    count = lax.axis_size(axis)
    results = []
    for start in (0, 1):
        pairs = [(i, i + 1) for i in range(start, count - 1, 2)]
        results.append(lax.ppermute(block, axis, pairs + [(j, i) for i, j in pairs]))
    return results


def after(value, *others):
    return lax.optimization_barrier((value, *others))[0]


def in_vmem(value):
    return pltpu.with_memory_space_constraint(value, pltpu.VMEM)


def local(volume, conv_weight, down_weight):
    bands = lax.axis_size("filt")
    count, planes, all_rows, width = volume.shape
    band = all_rows // bands
    window = BELOW + band + ABOVE
    half = width // 2
    hid_rows = band + 1
    vmem = pl.BlockSpec(memory_space=pltpu.VMEM)
    params = pltpu.CompilerParams(vmem_limit_bytes=VMEM_LIMIT)
    cost = pl.CostEstimate(flops=1, transcendentals=0, bytes_accessed=1)
    direct = count == 16 and bands == 4
    distances = (0, 1, 3, 2) if direct else ()
    ranges = [(0, 48), (0, 16), (16, 32), (48, 16)] if direct else [(0, C)]
    lay = pl.pallas_call(
        functools.partial(weight_kernel, distances, ranges),
        out_shape=[pltpu.VMEM((C2, 28 * C), jnp.bfloat16)]
        + [pltpu.VMEM((6 * C, 12 * channels), jnp.bfloat16) for _, channels in ranges],
        in_specs=[vmem] * 2,
        out_specs=[vmem] * (1 + len(ranges)),
        compiler_params=params,
        cost_estimate=cost,
    )
    def convolve(feature, groups, second=None):
        arrays = [] if feature is None else [feature]
        last = second is not None
        arrays += [second] if last else []
        for _, *given in groups:
            arrays += given
        kinds = [group for group, *_ in groups]
        scratch = [pltpu.VMEM((hid_rows * 9 * C, half), jnp.bfloat16)] * last
        for group in kinds:
            slots = 2 if group.inside else 4
            scratch.append(pltpu.VMEM((slots, window * 4 * group.channels, half), jnp.bfloat16))
        if last:
            shape = pltpu.VMEM((band // 2, C2, half), jnp.bfloat16)
        else:
            shape = pltpu.VMEM((hid_rows * 6 * C, half), jnp.float32)
        return pl.pallas_call(
            functools.partial(conv_kernel, kinds, window, feature is None, last),
            out_shape=shape,
            in_specs=[vmem] * len(arrays),
            out_specs=vmem,
            scratch_shapes=scratch,
            compiler_params=params,
            cost_estimate=pl.CostEstimate(flops=1 << 33, transcendentals=0, bytes_accessed=1 << 24),
        )(*map(in_vmem, arrays))

    if direct:
        step = 16
        sent = pl.pallas_call(
            functools.partial(send_kernel, band, distances),
            out_shape=[jax.ShapeDtypeStruct((window, planes, count, width), jnp.bfloat16)] * bands,
            in_specs=[pl.BlockSpec(memory_space=pltpu.HBM)],
            out_specs=[vmem] * bands,
            scratch_shapes=[
                pltpu.VMEM((planes * all_rows // step, count, step, width), jnp.bfloat16),
                pltpu.VMEM((BELOW + all_rows + ABOVE, planes, count, width), jnp.bfloat16),
                pltpu.SemaphoreType.DMA((planes * all_rows // step,)),
            ],
            compiler_params=params,
            cost_estimate=cost,
        )(pltpu.with_memory_space_constraint(volume, pltpu.HBM))
        second, *firsts = lay(conv_weight, down_weight)
        own = []
        for d, piece in zip(distances, sent):
            if d:
                piece = lax.ppermute(piece, "filt", [(i, i ^ d) for i in range(bands)])
            own.append(piece)
        mine = swapped(after(own[0], firsts[0]), "space")
        middle = pl.pallas_call(
            join_kernel,
            out_shape=pltpu.VMEM((2 * window, planes, count, width), jnp.bfloat16),
            in_specs=[vmem] * 2,
            out_specs=vmem,
            compiler_params=params,
            cost_estimate=cost,
        )(*map(in_vmem, own[1:3]))
        middles = swapped(middle, "space")
        all_three, of_own, of_middle, of_last = firsts
        feature = convolve(
            None,
            [
                (Group(True, 48, [(0, 0, 0), (1, 0, 16), (1, window, 32)]), all_three, own[0], middle),
                (Group(False, 16, [(0, 0, 0), (1, 0, 0)]), of_own, *mine),
            ],
        )
        tails = swapped(after(own[3], feature), "space")
        middles = [after(block, own[3]) for block in middles]
        in_middle = [(i, at * window, at * 16) for i in range(2) for at in range(2)]
        feature = convolve(
            feature,
            [
                (Group(True, 16, [(0, 0, 0)]), of_last, own[3]),
                (Group(False, 32, in_middle), of_middle, *middles),
            ],
        )
        coarse = convolve(feature, [(Group(False, 16, [(0, 0, 0), (1, 0, 0)]), of_last, *tails)], second)
    else:
        field = jnp.transpose(volume, (2, 1, 0, 3))
        field = jnp.concatenate([field[..., ::2], field[..., 1::2]], axis=-1)
        field = jnp.pad(field, ((BELOW, ABOVE), (0, 0), (0, 0), (0, 0)))
        sent = jnp.stack([field[t * band : t * band + window] for t in range(bands)])
        got = lax.all_to_all(sent, "filt", split_axis=0, concat_axis=0, tiled=True)
        own = jnp.transpose(got, (1, 2, 0, 3, 4)).reshape(window, planes, C, width)
        second, *firsts = lay(conv_weight, down_weight)
        inside = (Group(True, C, [(0, 0, 0)]), firsts[0], own)
        outside = (Group(False, C, [(0, 0, 0), (1, 0, 0)]), firsts[0], *swapped(own, "space"))
        coarse = convolve(None, [inside, outside], second)
    return jnp.transpose(coarse, (1, 0, 2))[:, None]


def solution(mesh):
    return jax.shard_map(
        local,
        mesh=mesh,
        in_specs=(P("filt", ("groups", "space"), None, None), P(), P()),
        out_specs=P(None, ("groups", "space"), "filt", None),
        check_vma=False,
    )
```

```python
import functools

import jax
import jax.numpy as jnp
from jax import lax
from jax.experimental import pallas as pl
from jax.experimental.pallas import tpu as pltpu
from jax.sharding import PartitionSpec as P

C = 64
C2 = 128
BELOW, ABOVE = 2, 1
negative_slope = 0.01
VMEM_LIMIT = 20 * 1024 * 1024


def split_matrix(width):
    half = width // 2
    source = lax.broadcasted_iota(jnp.int32, (width, width), 0)
    column = lax.broadcasted_iota(jnp.int32, (width, width), 1)
    wanted = jnp.where(column < half, 2 * column, 2 * (column - half) + 1)
    return jnp.where(source == wanted, 1.0, 0.0).astype(jnp.bfloat16)


def turn_matrix(count, rows):
    size = count * rows
    target = lax.broadcasted_iota(jnp.int32, (size, size), 0)
    source = lax.broadcasted_iota(jnp.int32, (size, size), 1)
    wanted = lax.rem(target, count) * rows + lax.div(target, count)
    return jnp.where(source == wanted, 1.0, 0.0).astype(jnp.bfloat16)


def send_kernel(band, distances, volume_ref, *refs):
    out_refs, (block_ref, field_ref, sems) = refs[:-3], refs[-3:]
    count, planes, all_rows, width = volume_ref.shape
    step = block_ref.shape[2]
    places = [(p, at) for at in range(0, all_rows, step) for p in range(planes)]
    copies = [
        pltpu.make_async_copy(volume_ref.at[:, p, pl.ds(at, step), :], block_ref.at[i], sems.at[i])
        for i, (p, at) in enumerate(places)
    ]
    for copy in copies:
        copy.start()
    part = width // 2
    split, turn = split_matrix(part), turn_matrix(count, step)
    field_ref[pl.ds(0, BELOW)] = jnp.zeros((BELOW, planes, count, width), jnp.bfloat16)
    field_ref[pl.ds(BELOW + all_rows, ABOVE)] = jnp.zeros((ABOVE, planes, count, width), jnp.bfloat16)
    for i, (p, at) in enumerate(places):
        copies[i].wait()
        block = block_ref[i].reshape(count * step, width)
        block = jnp.concatenate([block[:, :part], block[:, part:]])
        block = jnp.dot(block, split, preferred_element_type=jnp.float32).astype(jnp.bfloat16)
        left, right = block[: count * step], block[count * step :]
        cut = part // 2
        block = jnp.concatenate([left[:, :cut], right[:, :cut], left[:, cut:], right[:, cut:]], axis=1)
        block = jnp.dot(turn, block, preferred_element_type=jnp.float32).astype(jnp.bfloat16)
        field_ref[pl.ds(BELOW + at, step), p] = block.reshape(step, count, width)
    me = lax.axis_index("filt")
    for d, out_ref in zip(distances, out_refs):
        start = lax.bitwise_xor(me, d) * band
        out_ref[...] = field_ref[pl.ds(start, out_ref.shape[0])]


def store_taps(taps_ref, row, at, channels, cell):
    count, half = cell.shape[0], cell.shape[1] // 2
    lane = lax.broadcasted_iota(jnp.int32, (count, half), 1)
    even, odd = cell[:, :half], cell[:, half:]
    before = jnp.where(lane == 0, 0.0, pltpu.roll(odd.astype(jnp.float32), 1, 1))
    after_it = jnp.where(lane == half - 1, 0.0, pltpu.roll(even.astype(jnp.float32), half - 1, 1))
    for k, value in enumerate((before.astype(jnp.bfloat16), even, odd, after_it.astype(jnp.bfloat16))):
        taps_ref[pl.ds((4 * row + k) * channels + at, count), :] = value


def plane_parts(total, weight_ref, taps, y, p, depth):
    size = 2 * C
    z_low, z_high = max(0, p - 2), min(2, p)
    first = 2 - (p - z_low)
    weight = weight_ref[pl.ds(first * size, (z_high - z_low + 1) * size), :]
    part = jnp.dot(weight, taps[pl.ds(y * depth, 3 * depth), :], preferred_element_type=jnp.float32)
    for z in range(z_low, z_high + 1):
        piece = part[(z - z_low) * size : (z - z_low + 1) * size]
        total[z] = piece if total[z] is None else total[z] + piece


def join_kernel(one_ref, two_ref, out_ref):
    rows = one_ref.shape[0]
    out_ref[:rows] = one_ref[...]
    out_ref[rows:] = two_ref[...]


class Group:
    def __init__(self, inside, channels, blocks):
        self.inside, self.channels, self.blocks = inside, channels, blocks
        self.planes = (2, 3) if inside else (0, 1, 4)
        self.arrays = 1 + max(i for i, _, _ in blocks)


def conv_kernel(groups, window, first, last, *refs):
    space, band = lax.axis_index("space"), lax.axis_index("filt")
    odd = lax.rem(space, 2)
    places = ((2 - 2 * odd, 3 - 2 * odd), (2 * odd, 1 + 2 * odd))
    refs = list(refs)
    feature_ref = None if first else refs.pop(0)
    second_ref = refs.pop(0) if last else None
    inputs = [[refs.pop(0) for _ in range(1 + group.arrays)] for group in groups]
    out_ref = refs.pop(0)
    hid_ref = refs.pop(0) if last else None
    half = out_ref.shape[-1]
    for group, (_, *blocks), taps_ref in zip(groups, inputs, refs):
        for i, row, at in group.blocks:
            for r in range(window):
                for k in range(2):
                    place = k if group.inside else places[i % 2][k]
                    store_taps(taps_ref.at[place], r, at, group.channels, blocks[i][row + r, k])
    size = 2 * C
    lane = lax.broadcasted_iota(jnp.int32, (C, half), 1)
    for y in range(window - 2):
        total = [None if first else feature_ref[pl.ds((y * 3 + z) * size, size), :] for z in range(3)]
        for group, (weight_ref, *_), taps_ref in zip(groups, inputs, refs):
            for k, p in enumerate(group.planes):
                plane_parts(total, weight_ref, taps_ref.at[k], y, p, 4 * group.channels)
        for z in range(3):
            if not last:
                out_ref[pl.ds((y * 3 + z) * size, size), :] = total[z]
                continue
            value = total[z]
            value = jnp.where(value > 0, value, negative_slope * value)
            if z == 0:
                value = jnp.where(space > 0, value, 0.0)
            if y == 0:
                value = jnp.where(band > 0, value, 0.0)
            value = value.astype(jnp.bfloat16)
            before = jnp.where(lane == 0, 0.0, pltpu.roll(value[C:].astype(jnp.float32), 1, 1))
            base = (y * 3 + z) * 3 * C
            hid_ref[pl.ds(base, C), :] = before.astype(jnp.bfloat16)
            hid_ref[pl.ds(base + C, 2 * C), :] = value
    if last:
        for y in range(out_ref.shape[0]):
            out_ref[y] = jnp.dot(
                second_ref[:, : 27 * C],
                hid_ref[pl.ds(2 * y * 9 * C, 27 * C), :],
                preferred_element_type=jnp.float32,
            ).astype(jnp.bfloat16)


def exact(left, right):
    return jnp.dot(left, right, preferred_element_type=jnp.float32)


def weight_kernel(distances, ranges, conv_ref, down_ref, second_ref, *first_refs):
    row = lax.broadcasted_iota(jnp.int32, (2 * C, 2 * C), 0)
    lane = lax.broadcasted_iota(jnp.int32, (2 * C, 2 * C), 1)
    hidden = 2 * lax.rem(lane, C // 2) + lax.div(lax.rem(lane, C), C // 2)
    pair = [
        [((row == C * odd + hidden) & (lax.div(lane, C) == k)).astype(jnp.bfloat16) for k in range(2)]
        for odd in range(2)
    ]
    in_order = (row == 2 * lax.rem(lane, C) + lax.div(lane, C)).astype(jnp.bfloat16)
    down = [[down_ref[a, b].reshape(3, C, 2 * C) for b in range(3)] for a in range(3)]
    for j in range(14):
        halves = []
        for odd in range(2):
            total = None
            for k in range(2):
                t = 2 * j + k
                if t < 27:
                    part = exact(down[t // 3 % 3][t // 9][t % 3], pair[odd][k])
                    total = part if total is None else total + part
            halves.append(total.astype(jnp.bfloat16))
        second_ref[:, pl.ds(2 * C * j, 2 * C)] = exact(in_order, jnp.concatenate(halves)).astype(jnp.bfloat16)
    conv = [[conv_ref[a, b].reshape(3, C // 2, 2 * C) for b in range(3)] for a in range(3)]
    taps = [[jnp.concatenate([conv[a][b][c] for a in range(3)]) for c in range(3)] for b in range(3)]
    for (start, channels), first_ref in zip(ranges, first_refs):
        row = lax.broadcasted_iota(jnp.int32, (2 * C, 12 * channels), 0)
        lane = lax.broadcasted_iota(jnp.int32, (2 * C, 12 * channels), 1)
        place = start + lax.rem(lane, channels)
        source = place
        if distances:
            me, count = lax.axis_index("filt"), C // len(distances)
            for i, d in enumerate(distances):
                moved = lax.bitwise_xor(me, d) * count + place - i * count
                source = jnp.where(lax.div(place, count) == i, moved, source)
        for odd in range(2):
            shift = jnp.where(row == C * odd + source, lax.div(lane, channels), -1)
            for parity in range(2):
                total = None
                for b in range(3):
                    for c in range(3):
                        part = exact(taps[b][c], (shift == 4 * b + c + parity).astype(jnp.bfloat16))
                        total = part if total is None else total + part
                total = total.astype(jnp.bfloat16)
                for a in range(3):
                    at = (2 - a) * 2 * C + parity * C + odd * C // 2
                    first_ref[pl.ds(at, C // 2), :] = total[a * C // 2 : (a + 1) * C // 2]


def swapped(block, axis):
    count = lax.axis_size(axis)
    results = []
    for start in (0, 1):
        pairs = [(i, i + 1) for i in range(start, count - 1, 2)]
        results.append(lax.ppermute(block, axis, pairs + [(j, i) for i, j in pairs]))
    return results


def after(value, *others):
    return lax.optimization_barrier((value, *others))[0]


def in_vmem(value):
    return pltpu.with_memory_space_constraint(value, pltpu.VMEM)


def local(volume, conv_weight, down_weight):
    bands = lax.axis_size("filt")
    count, planes, all_rows, width = volume.shape
    band = all_rows // bands
    window = BELOW + band + ABOVE
    half = width // 2
    hid_rows = band + 1
    vmem = pl.BlockSpec(memory_space=pltpu.VMEM)
    params = pltpu.CompilerParams(vmem_limit_bytes=VMEM_LIMIT)
    cost = pl.CostEstimate(flops=1, transcendentals=0, bytes_accessed=1)
    direct = count == 16 and bands == 4
    distances = (0, 3, 1, 2) if direct else ()
    ranges = [(0, 48), (0, 16), (16, 32), (48, 16)] if direct else [(0, C)]
    lay = pl.pallas_call(
        functools.partial(weight_kernel, distances, ranges),
        out_shape=[pltpu.VMEM((C2, 28 * C), jnp.bfloat16)]
        + [pltpu.VMEM((6 * C, 12 * channels), jnp.bfloat16) for _, channels in ranges],
        in_specs=[vmem] * 2,
        out_specs=[vmem] * (1 + len(ranges)),
        compiler_params=params,
        cost_estimate=cost,
    )
    def convolve(feature, groups, second=None):
        arrays = [] if feature is None else [feature]
        last = second is not None
        arrays += [second] if last else []
        for _, *given in groups:
            arrays += given
        kinds = [group for group, *_ in groups]
        scratch = [pltpu.VMEM((hid_rows * 9 * C, half), jnp.bfloat16)] * last
        for group in kinds:
            slots = 2 if group.inside else 4
            scratch.append(pltpu.VMEM((slots, window * 4 * group.channels, half), jnp.bfloat16))
        if last:
            shape = pltpu.VMEM((band // 2, C2, half), jnp.bfloat16)
        else:
            shape = pltpu.VMEM((hid_rows * 6 * C, half), jnp.float32)
        return pl.pallas_call(
            functools.partial(conv_kernel, kinds, window, feature is None, last),
            out_shape=shape,
            in_specs=[vmem] * len(arrays),
            out_specs=vmem,
            scratch_shapes=scratch,
            compiler_params=params,
            cost_estimate=pl.CostEstimate(flops=1 << 33, transcendentals=0, bytes_accessed=1 << 24),
        )(*map(in_vmem, arrays))

    if direct:
        step = 16
        sent = pl.pallas_call(
            functools.partial(send_kernel, band, distances),
            out_shape=[jax.ShapeDtypeStruct((window, planes, count, width), jnp.bfloat16)] * bands,
            in_specs=[pl.BlockSpec(memory_space=pltpu.HBM)],
            out_specs=[vmem] * bands,
            scratch_shapes=[
                pltpu.VMEM((planes * all_rows // step, count, step, width), jnp.bfloat16),
                pltpu.VMEM((BELOW + all_rows + ABOVE, planes, count, width), jnp.bfloat16),
                pltpu.SemaphoreType.DMA((planes * all_rows // step,)),
            ],
            compiler_params=params,
            cost_estimate=cost,
        )(pltpu.with_memory_space_constraint(volume, pltpu.HBM))
        second, *firsts = lay(conv_weight, down_weight)
        own = []
        for d, piece in zip(distances, sent):
            if d:
                piece = lax.ppermute(piece, "filt", [(i, i ^ d) for i in range(bands)])
            own.append(piece)
        mine = swapped(after(own[0], firsts[0]), "space")
        middle = pl.pallas_call(
            join_kernel,
            out_shape=pltpu.VMEM((2 * window, planes, count, width), jnp.bfloat16),
            in_specs=[vmem] * 2,
            out_specs=vmem,
            compiler_params=params,
            cost_estimate=cost,
        )(*map(in_vmem, own[1:3]))
        middles = swapped(middle, "space")
        all_three, of_own, of_middle, of_last = firsts
        feature = convolve(
            None,
            [
                (Group(True, 48, [(0, 0, 0), (1, 0, 16), (1, window, 32)]), all_three, own[0], middle),
                (Group(False, 16, [(0, 0, 0), (1, 0, 0)]), of_own, *mine),
            ],
        )
        tails = swapped(after(own[3], feature), "space")
        middles = [after(block, own[3]) for block in middles]
        in_middle = [(i, at * window, at * 16) for i in range(2) for at in range(2)]
        feature = convolve(
            feature,
            [
                (Group(True, 16, [(0, 0, 0)]), of_last, own[3]),
                (Group(False, 32, in_middle), of_middle, *middles),
            ],
        )
        coarse = convolve(feature, [(Group(False, 16, [(0, 0, 0), (1, 0, 0)]), of_last, *tails)], second)
    else:
        field = jnp.transpose(volume, (2, 1, 0, 3))
        field = jnp.concatenate([field[..., ::2], field[..., 1::2]], axis=-1)
        field = jnp.pad(field, ((BELOW, ABOVE), (0, 0), (0, 0), (0, 0)))
        sent = jnp.stack([field[t * band : t * band + window] for t in range(bands)])
        got = lax.all_to_all(sent, "filt", split_axis=0, concat_axis=0, tiled=True)
        own = jnp.transpose(got, (1, 2, 0, 3, 4)).reshape(window, planes, C, width)
        second, *firsts = lay(conv_weight, down_weight)
        inside = (Group(True, C, [(0, 0, 0)]), firsts[0], own)
        outside = (Group(False, C, [(0, 0, 0), (1, 0, 0)]), firsts[0], *swapped(own, "space"))
        coarse = convolve(None, [inside, outside], second)
    return jnp.transpose(coarse, (1, 0, 2))[:, None]


def solution(mesh):
    return jax.shard_map(
        local,
        mesh=mesh,
        in_specs=(P("filt", ("groups", "space"), None, None), P(), P()),
        out_specs=P(None, ("groups", "space"), "filt", None),
        check_vma=False,
    )
```

```python
import functools

import jax
import jax.numpy as jnp
from jax import lax
from jax.experimental import pallas as pl
from jax.experimental.pallas import tpu as pltpu
from jax.sharding import PartitionSpec as P

C = 64
C2 = 128
BELOW, ABOVE = 2, 1
negative_slope = 0.01
VMEM_LIMIT = 20 * 1024 * 1024


def split_matrix(width):
    half = width // 2
    source = lax.broadcasted_iota(jnp.int32, (width, width), 0)
    column = lax.broadcasted_iota(jnp.int32, (width, width), 1)
    wanted = jnp.where(column < half, 2 * column, 2 * (column - half) + 1)
    return jnp.where(source == wanted, 1.0, 0.0).astype(jnp.bfloat16)


def turn_matrix(count, rows):
    size = count * rows
    target = lax.broadcasted_iota(jnp.int32, (size, size), 0)
    source = lax.broadcasted_iota(jnp.int32, (size, size), 1)
    wanted = lax.rem(target, count) * rows + lax.div(target, count)
    return jnp.where(source == wanted, 1.0, 0.0).astype(jnp.bfloat16)


def send_kernel(band, distances, volume_ref, *refs):
    out_refs, (block_ref, field_ref, sems) = refs[:-3], refs[-3:]
    count, planes, all_rows, width = volume_ref.shape
    step = block_ref.shape[2]
    places = [(p, at) for at in range(0, all_rows, step) for p in range(planes)]
    copies = [
        pltpu.make_async_copy(volume_ref.at[:, p, pl.ds(at, step), :], block_ref.at[i], sems.at[i])
        for i, (p, at) in enumerate(places)
    ]
    for copy in copies:
        copy.start()
    turn = turn_matrix(count, step)
    field_ref[pl.ds(0, BELOW)] = jnp.zeros((BELOW, planes, count, width), jnp.bfloat16)
    field_ref[pl.ds(BELOW + all_rows, ABOVE)] = jnp.zeros((ABOVE, planes, count, width), jnp.bfloat16)
    for copy in copies:
        copy.wait()
    size = count * step
    wide = jnp.concatenate([block_ref[i].reshape(size, width) for i in range(len(places))], axis=1)
    wide = jnp.dot(turn, wide, preferred_element_type=jnp.float32).astype(jnp.bfloat16)
    tall = jnp.concatenate([wide[:, i * width // 2 : (i + 1) * width // 2] for i in range(2 * len(places))])
    tall = jnp.dot(tall, split_matrix(width // 2), preferred_element_type=jnp.float32).astype(jnp.bfloat16)
    cut = width // 4
    for i, (p, at) in enumerate(places):
        left, right = tall[2 * i * size : (2 * i + 1) * size], tall[(2 * i + 1) * size : (2 * i + 2) * size]
        block = jnp.concatenate([left[:, :cut], right[:, :cut], left[:, cut:], right[:, cut:]], axis=1)
        field_ref[pl.ds(BELOW + at, step), p] = block.reshape(step, count, width)
    me = lax.axis_index("filt")
    for d, out_ref in zip(distances, out_refs):
        start = lax.bitwise_xor(me, d) * band
        out_ref[...] = field_ref[pl.ds(start, out_ref.shape[0])]


def store_taps(taps_ref, row, at, channels, cell):
    count, half = cell.shape[0], cell.shape[1] // 2
    lane = lax.broadcasted_iota(jnp.int32, (count, half), 1)
    even, odd = cell[:, :half], cell[:, half:]
    before = jnp.where(lane == 0, 0.0, pltpu.roll(odd.astype(jnp.float32), 1, 1))
    after_it = jnp.where(lane == half - 1, 0.0, pltpu.roll(even.astype(jnp.float32), half - 1, 1))
    for k, value in enumerate((before.astype(jnp.bfloat16), even, odd, after_it.astype(jnp.bfloat16))):
        taps_ref[pl.ds((4 * row + k) * channels + at, count), :] = value


def plane_parts(total, weight_ref, taps, y, p, depth):
    size = 2 * C
    z_low, z_high = max(0, p - 2), min(2, p)
    first = 2 - (p - z_low)
    weight = weight_ref[pl.ds(first * size, (z_high - z_low + 1) * size), :]
    part = jnp.dot(weight, taps[pl.ds(y * depth, 3 * depth), :], preferred_element_type=jnp.float32)
    for z in range(z_low, z_high + 1):
        piece = part[(z - z_low) * size : (z - z_low + 1) * size]
        total[z] = piece if total[z] is None else total[z] + piece


def join_kernel(one_ref, two_ref, out_ref):
    rows = one_ref.shape[0]
    out_ref[:rows] = one_ref[...]
    out_ref[rows:] = two_ref[...]


class Group:
    def __init__(self, inside, channels, blocks):
        self.inside, self.channels, self.blocks = inside, channels, blocks
        self.planes = (2, 3) if inside else (0, 1, 4)
        self.arrays = 1 + max(i for i, _, _ in blocks)


def conv_kernel(groups, window, first, last, *refs):
    space, band = lax.axis_index("space"), lax.axis_index("filt")
    odd = lax.rem(space, 2)
    places = ((2 - 2 * odd, 3 - 2 * odd), (2 * odd, 1 + 2 * odd))
    refs = list(refs)
    feature_ref = None if first else refs.pop(0)
    second_ref = refs.pop(0) if last else None
    inputs = [[refs.pop(0) for _ in range(1 + group.arrays)] for group in groups]
    out_ref = refs.pop(0)
    hid_ref = refs.pop(0) if last else None
    half = out_ref.shape[-1]
    for group, (_, *blocks), taps_ref in zip(groups, inputs, refs):
        for i, row, at in group.blocks:
            for r in range(window):
                for k in range(2):
                    place = k if group.inside else places[i % 2][k]
                    store_taps(taps_ref.at[place], r, at, group.channels, blocks[i][row + r, k])
    size = 2 * C
    lane = lax.broadcasted_iota(jnp.int32, (C, half), 1)
    for y in range(window - 2):
        total = [None if first else feature_ref[pl.ds((y * 3 + z) * size, size), :] for z in range(3)]
        for group, (weight_ref, *_), taps_ref in zip(groups, inputs, refs):
            for k, p in enumerate(group.planes):
                plane_parts(total, weight_ref, taps_ref.at[k], y, p, 4 * group.channels)
        for z in range(3):
            if not last:
                out_ref[pl.ds((y * 3 + z) * size, size), :] = total[z]
                continue
            value = total[z]
            value = jnp.where(value > 0, value, negative_slope * value)
            if z == 0:
                value = jnp.where(space > 0, value, 0.0)
            if y == 0:
                value = jnp.where(band > 0, value, 0.0)
            value = value.astype(jnp.bfloat16)
            before = jnp.where(lane == 0, 0.0, pltpu.roll(value[C:].astype(jnp.float32), 1, 1))
            base = (y * 3 + z) * 3 * C
            hid_ref[pl.ds(base, C), :] = before.astype(jnp.bfloat16)
            hid_ref[pl.ds(base + C, 2 * C), :] = value
    if last:
        for y in range(out_ref.shape[0]):
            out_ref[y] = jnp.dot(
                second_ref[:, : 27 * C],
                hid_ref[pl.ds(2 * y * 9 * C, 27 * C), :],
                preferred_element_type=jnp.float32,
            ).astype(jnp.bfloat16)


def exact(left, right):
    return jnp.dot(left, right, preferred_element_type=jnp.float32)


def weight_kernel(distances, ranges, conv_ref, down_ref, second_ref, *first_refs):
    row = lax.broadcasted_iota(jnp.int32, (2 * C, 2 * C), 0)
    lane = lax.broadcasted_iota(jnp.int32, (2 * C, 2 * C), 1)
    hidden = 2 * lax.rem(lane, C // 2) + lax.div(lax.rem(lane, C), C // 2)
    pair = [
        [((row == C * odd + hidden) & (lax.div(lane, C) == k)).astype(jnp.bfloat16) for k in range(2)]
        for odd in range(2)
    ]
    in_order = (row == 2 * lax.rem(lane, C) + lax.div(lane, C)).astype(jnp.bfloat16)
    down = [[down_ref[a, b].reshape(3, C, 2 * C) for b in range(3)] for a in range(3)]
    for j in range(14):
        halves = []
        for odd in range(2):
            total = None
            for k in range(2):
                t = 2 * j + k
                if t < 27:
                    part = exact(down[t // 3 % 3][t // 9][t % 3], pair[odd][k])
                    total = part if total is None else total + part
            halves.append(total.astype(jnp.bfloat16))
        second_ref[:, pl.ds(2 * C * j, 2 * C)] = exact(in_order, jnp.concatenate(halves)).astype(jnp.bfloat16)
    conv = [[conv_ref[a, b].reshape(3, C // 2, 2 * C) for b in range(3)] for a in range(3)]
    taps = [[jnp.concatenate([conv[a][b][c] for a in range(3)]) for c in range(3)] for b in range(3)]
    for (start, channels), first_ref in zip(ranges, first_refs):
        row = lax.broadcasted_iota(jnp.int32, (2 * C, 12 * channels), 0)
        lane = lax.broadcasted_iota(jnp.int32, (2 * C, 12 * channels), 1)
        place = start + lax.rem(lane, channels)
        source = place
        if distances:
            me, count = lax.axis_index("filt"), C // len(distances)
            for i, d in enumerate(distances):
                moved = lax.bitwise_xor(me, d) * count + place - i * count
                source = jnp.where(lax.div(place, count) == i, moved, source)
        for odd in range(2):
            shift = jnp.where(row == C * odd + source, lax.div(lane, channels), -1)
            for parity in range(2):
                total = None
                for b in range(3):
                    for c in range(3):
                        part = exact(taps[b][c], (shift == 4 * b + c + parity).astype(jnp.bfloat16))
                        total = part if total is None else total + part
                total = total.astype(jnp.bfloat16)
                for a in range(3):
                    at = (2 - a) * 2 * C + parity * C + odd * C // 2
                    first_ref[pl.ds(at, C // 2), :] = total[a * C // 2 : (a + 1) * C // 2]


def swapped(block, axis):
    count = lax.axis_size(axis)
    results = []
    for start in (0, 1):
        pairs = [(i, i + 1) for i in range(start, count - 1, 2)]
        results.append(lax.ppermute(block, axis, pairs + [(j, i) for i, j in pairs]))
    return results


def after(value, *others):
    return lax.optimization_barrier((value, *others))[0]


def in_vmem(value):
    return pltpu.with_memory_space_constraint(value, pltpu.VMEM)


def local(volume, conv_weight, down_weight):
    bands = lax.axis_size("filt")
    count, planes, all_rows, width = volume.shape
    band = all_rows // bands
    window = BELOW + band + ABOVE
    half = width // 2
    hid_rows = band + 1
    vmem = pl.BlockSpec(memory_space=pltpu.VMEM)
    params = pltpu.CompilerParams(vmem_limit_bytes=VMEM_LIMIT)
    cost = pl.CostEstimate(flops=1, transcendentals=0, bytes_accessed=1)
    direct = count == 16 and bands == 4
    distances = (0, 3, 1, 2) if direct else ()
    ranges = [(0, 48), (0, 16), (16, 32), (48, 16)] if direct else [(0, C)]
    lay = pl.pallas_call(
        functools.partial(weight_kernel, distances, ranges),
        out_shape=[pltpu.VMEM((C2, 28 * C), jnp.bfloat16)]
        + [pltpu.VMEM((6 * C, 12 * channels), jnp.bfloat16) for _, channels in ranges],
        in_specs=[vmem] * 2,
        out_specs=[vmem] * (1 + len(ranges)),
        compiler_params=params,
        cost_estimate=cost,
    )
    def convolve(feature, groups, second=None):
        arrays = [] if feature is None else [feature]
        last = second is not None
        arrays += [second] if last else []
        for _, *given in groups:
            arrays += given
        kinds = [group for group, *_ in groups]
        scratch = [pltpu.VMEM((hid_rows * 9 * C, half), jnp.bfloat16)] * last
        for group in kinds:
            slots = 2 if group.inside else 4
            scratch.append(pltpu.VMEM((slots, window * 4 * group.channels, half), jnp.bfloat16))
        if last:
            shape = pltpu.VMEM((band // 2, C2, half), jnp.bfloat16)
        else:
            shape = pltpu.VMEM((hid_rows * 6 * C, half), jnp.float32)
        return pl.pallas_call(
            functools.partial(conv_kernel, kinds, window, feature is None, last),
            out_shape=shape,
            in_specs=[vmem] * len(arrays),
            out_specs=vmem,
            scratch_shapes=scratch,
            compiler_params=params,
            cost_estimate=pl.CostEstimate(flops=1 << 33, transcendentals=0, bytes_accessed=1 << 24),
        )(*map(in_vmem, arrays))

    if direct:
        step = 16
        sent = pl.pallas_call(
            functools.partial(send_kernel, band, distances),
            out_shape=[jax.ShapeDtypeStruct((window, planes, count, width), jnp.bfloat16)] * bands,
            in_specs=[pl.BlockSpec(memory_space=pltpu.HBM)],
            out_specs=[vmem] * bands,
            scratch_shapes=[
                pltpu.VMEM((planes * all_rows // step, count, step, width), jnp.bfloat16),
                pltpu.VMEM((BELOW + all_rows + ABOVE, planes, count, width), jnp.bfloat16),
                pltpu.SemaphoreType.DMA((planes * all_rows // step,)),
            ],
            compiler_params=params,
            cost_estimate=cost,
        )(pltpu.with_memory_space_constraint(volume, pltpu.HBM))
        second, *firsts = lay(conv_weight, down_weight)
        own = []
        for d, piece in zip(distances, sent):
            if d:
                piece = lax.ppermute(piece, "filt", [(i, i ^ d) for i in range(bands)])
            own.append(piece)
        mine = swapped(after(own[0], firsts[0]), "space")
        middle = pl.pallas_call(
            join_kernel,
            out_shape=pltpu.VMEM((2 * window, planes, count, width), jnp.bfloat16),
            in_specs=[vmem] * 2,
            out_specs=vmem,
            compiler_params=params,
            cost_estimate=cost,
        )(*map(in_vmem, own[1:3]))
        middles = swapped(middle, "space")
        all_three, of_own, of_middle, of_last = firsts
        feature = convolve(
            None,
            [
                (Group(True, 48, [(0, 0, 0), (1, 0, 16), (1, window, 32)]), all_three, own[0], middle),
                (Group(False, 16, [(0, 0, 0), (1, 0, 0)]), of_own, *mine),
            ],
        )
        tails = swapped(after(own[3], feature), "space")
        middles = [after(block, own[3]) for block in middles]
        in_middle = [(i, at * window, at * 16) for i in range(2) for at in range(2)]
        feature = convolve(
            feature,
            [
                (Group(True, 16, [(0, 0, 0)]), of_last, own[3]),
                (Group(False, 32, in_middle), of_middle, *middles),
            ],
        )
        coarse = convolve(feature, [(Group(False, 16, [(0, 0, 0), (1, 0, 0)]), of_last, *tails)], second)
    else:
        field = jnp.transpose(volume, (2, 1, 0, 3))
        field = jnp.concatenate([field[..., ::2], field[..., 1::2]], axis=-1)
        field = jnp.pad(field, ((BELOW, ABOVE), (0, 0), (0, 0), (0, 0)))
        sent = jnp.stack([field[t * band : t * band + window] for t in range(bands)])
        got = lax.all_to_all(sent, "filt", split_axis=0, concat_axis=0, tiled=True)
        own = jnp.transpose(got, (1, 2, 0, 3, 4)).reshape(window, planes, C, width)
        second, *firsts = lay(conv_weight, down_weight)
        inside = (Group(True, C, [(0, 0, 0)]), firsts[0], own)
        outside = (Group(False, C, [(0, 0, 0), (1, 0, 0)]), firsts[0], *swapped(own, "space"))
        coarse = convolve(None, [inside, outside], second)
    return jnp.transpose(coarse, (1, 0, 2))[:, None]


def solution(mesh):
    return jax.shard_map(
        local,
        mesh=mesh,
        in_specs=(P("filt", ("groups", "space"), None, None), P(), P()),
        out_specs=P(None, ("groups", "space"), "filt", None),
        check_vma=False,
    )
```

```python
import functools

import jax
import jax.numpy as jnp
from jax import lax
from jax.experimental import pallas as pl
from jax.experimental.pallas import tpu as pltpu
from jax.sharding import PartitionSpec as P

C = 64
C2 = 128
BELOW, ABOVE = 2, 1
negative_slope = 0.01
VMEM_LIMIT = 20 * 1024 * 1024


def split_matrix(width):
    half = width // 2
    source = lax.broadcasted_iota(jnp.int32, (width, width), 0)
    column = lax.broadcasted_iota(jnp.int32, (width, width), 1)
    wanted = jnp.where(column < half, 2 * column, 2 * (column - half) + 1)
    return jnp.where(source == wanted, 1.0, 0.0).astype(jnp.bfloat16)


def turn_matrix(count, rows):
    size = count * rows
    target = lax.broadcasted_iota(jnp.int32, (size, size), 0)
    source = lax.broadcasted_iota(jnp.int32, (size, size), 1)
    wanted = lax.rem(target, count) * rows + lax.div(target, count)
    return jnp.where(source == wanted, 1.0, 0.0).astype(jnp.bfloat16)


def send_kernel(band, parts, volume_ref, *refs):
    out_refs, (block_ref, field_ref, sems) = refs[:-3], refs[-3:]
    count, planes, all_rows, width = volume_ref.shape
    step = block_ref.shape[2]
    places = [(p, at) for at in range(0, all_rows, step) for p in range(planes)]
    copies = [
        pltpu.make_async_copy(volume_ref.at[:, p, pl.ds(at, step), :], block_ref.at[i], sems.at[i])
        for i, (p, at) in enumerate(places)
    ]
    for copy in copies:
        copy.start()
    turn = turn_matrix(count, step)
    field_ref[pl.ds(0, BELOW)] = jnp.zeros((BELOW, planes, count, width), jnp.bfloat16)
    field_ref[pl.ds(BELOW + all_rows, ABOVE)] = jnp.zeros((ABOVE, planes, count, width), jnp.bfloat16)
    for copy in copies:
        copy.wait()
    size = count * step
    wide = jnp.concatenate([block_ref[i].reshape(size, width) for i in range(len(places))], axis=1)
    wide = jnp.dot(turn, wide, preferred_element_type=jnp.float32).astype(jnp.bfloat16)
    tall = jnp.concatenate([wide[:, i * width // 2 : (i + 1) * width // 2] for i in range(2 * len(places))])
    tall = jnp.dot(tall, split_matrix(width // 2), preferred_element_type=jnp.float32).astype(jnp.bfloat16)
    cut = width // 4
    for i, (p, at) in enumerate(places):
        left, right = tall[2 * i * size : (2 * i + 1) * size], tall[(2 * i + 1) * size : (2 * i + 2) * size]
        block = jnp.concatenate([left[:, :cut], right[:, :cut], left[:, cut:], right[:, cut:]], axis=1)
        field_ref[pl.ds(BELOW + at, step), p] = block.reshape(step, count, width)
    me = lax.axis_index("filt")
    for (d, low, _), out_ref in zip(parts, out_refs):
        start = lax.bitwise_xor(me, d) * band + low
        out_ref[...] = field_ref[pl.ds(start, out_ref.shape[0])]


def store_taps(taps_ref, row, at, channels, cell):
    count, half = cell.shape[0], cell.shape[1] // 2
    lane = lax.broadcasted_iota(jnp.int32, (count, half), 1)
    even, odd = cell[:, :half], cell[:, half:]
    before = jnp.where(lane == 0, 0.0, pltpu.roll(odd.astype(jnp.float32), 1, 1))
    after_it = jnp.where(lane == half - 1, 0.0, pltpu.roll(even.astype(jnp.float32), half - 1, 1))
    for k, value in enumerate((before.astype(jnp.bfloat16), even, odd, after_it.astype(jnp.bfloat16))):
        taps_ref[pl.ds((4 * row + k) * channels + at, count), :] = value


def plane_parts(total, weight_ref, taps, y, p, depth):
    size = 2 * C
    z_low, z_high = max(0, p - 2), min(2, p)
    first = 2 - (p - z_low)
    weight = weight_ref[pl.ds(first * size, (z_high - z_low + 1) * size), :]
    part = jnp.dot(weight, taps[pl.ds(y * depth, 3 * depth), :], preferred_element_type=jnp.float32)
    for z in range(z_low, z_high + 1):
        piece = part[(z - z_low) * size : (z - z_low + 1) * size]
        total[z] = piece if total[z] is None else total[z] + piece


def join_kernel(one_ref, two_ref, out_ref):
    rows = one_ref.shape[0]
    out_ref[:rows] = one_ref[...]
    out_ref[rows:] = two_ref[...]


class Group:
    def __init__(self, inside, channels, blocks):
        self.inside, self.channels, self.blocks = inside, channels, blocks
        self.planes = (2, 3) if inside else (0, 1, 4)
        self.arrays = 1 + max(block[0] for block in blocks)


def conv_kernel(groups, window, first, last, *refs):
    space, band = lax.axis_index("space"), lax.axis_index("filt")
    odd = lax.rem(space, 2)
    places = ((2 * odd, 1 + 2 * odd), (2 - 2 * odd, 3 - 2 * odd))
    refs = list(refs)
    feature_ref = None if first else refs.pop(0)
    second_ref = refs.pop(0) if last else None
    inputs = [[refs.pop(0) for _ in range(1 + group.arrays)] for group in groups]
    out_ref = refs.pop(0)
    hid_ref = refs.pop(0) if last else None
    half = out_ref.shape[-1]
    for group, (_, *blocks), taps_ref in zip(groups, inputs, refs):
        for i, row, at, low, high in group.blocks:
            for r in range(low, high):
                for k in range(2):
                    place = k if group.inside else places[i % 2][k]
                    store_taps(taps_ref.at[place], r, at, group.channels, blocks[i][row + r - low, k])
    size = 2 * C
    lane = lax.broadcasted_iota(jnp.int32, (C, half), 1)
    for y in range(window - 2):
        total = [None if first else feature_ref[pl.ds((y * 3 + z) * size, size), :] for z in range(3)]
        for group, (weight_ref, *_), taps_ref in zip(groups, inputs, refs):
            for k, p in enumerate(group.planes):
                plane_parts(total, weight_ref, taps_ref.at[k], y, p, 4 * group.channels)
        for z in range(3):
            if not last:
                out_ref[pl.ds((y * 3 + z) * size, size), :] = total[z]
                continue
            value = total[z]
            value = jnp.where(value > 0, value, negative_slope * value)
            if z == 0:
                value = jnp.where(space > 0, value, 0.0)
            if y == 0:
                value = jnp.where(band > 0, value, 0.0)
            value = value.astype(jnp.bfloat16)
            before = jnp.where(lane == 0, 0.0, pltpu.roll(value[C:].astype(jnp.float32), 1, 1))
            base = (y * 3 + z) * 3 * C
            hid_ref[pl.ds(base, C), :] = before.astype(jnp.bfloat16)
            hid_ref[pl.ds(base + C, 2 * C), :] = value
    if last:
        for y in range(out_ref.shape[0]):
            out_ref[y] = jnp.dot(
                second_ref[:, : 27 * C],
                hid_ref[pl.ds(2 * y * 9 * C, 27 * C), :],
                preferred_element_type=jnp.float32,
            ).astype(jnp.bfloat16)


def exact(left, right):
    return jnp.dot(left, right, preferred_element_type=jnp.float32)


def weight_kernel(distances, ranges, conv_ref, down_ref, second_ref, *first_refs):
    row = lax.broadcasted_iota(jnp.int32, (2 * C, 2 * C), 0)
    lane = lax.broadcasted_iota(jnp.int32, (2 * C, 2 * C), 1)
    hidden = 2 * lax.rem(lane, C // 2) + lax.div(lax.rem(lane, C), C // 2)
    pair = [
        [((row == C * odd + hidden) & (lax.div(lane, C) == k)).astype(jnp.bfloat16) for k in range(2)]
        for odd in range(2)
    ]
    in_order = (row == 2 * lax.rem(lane, C) + lax.div(lane, C)).astype(jnp.bfloat16)
    down = [[down_ref[a, b].reshape(3, C, 2 * C) for b in range(3)] for a in range(3)]
    for j in range(14):
        halves = []
        for odd in range(2):
            total = None
            for k in range(2):
                t = 2 * j + k
                if t < 27:
                    part = exact(down[t // 3 % 3][t // 9][t % 3], pair[odd][k])
                    total = part if total is None else total + part
            halves.append(total.astype(jnp.bfloat16))
        second_ref[:, pl.ds(2 * C * j, 2 * C)] = exact(in_order, jnp.concatenate(halves)).astype(jnp.bfloat16)
    conv = [[conv_ref[a, b].reshape(3, C // 2, 2 * C) for b in range(3)] for a in range(3)]
    taps = [[jnp.concatenate([conv[a][b][c] for a in range(3)]) for c in range(3)] for b in range(3)]
    for (start, channels), first_ref in zip(ranges, first_refs):
        row = lax.broadcasted_iota(jnp.int32, (2 * C, 12 * channels), 0)
        lane = lax.broadcasted_iota(jnp.int32, (2 * C, 12 * channels), 1)
        place = start + lax.rem(lane, channels)
        source = place
        if distances:
            me, count = lax.axis_index("filt"), C // len(distances)
            for i, d in enumerate(distances):
                moved = lax.bitwise_xor(me, d) * count + place - i * count
                source = jnp.where(lax.div(place, count) == i, moved, source)
        for odd in range(2):
            shift = jnp.where(row == C * odd + source, lax.div(lane, channels), -1)
            for parity in range(2):
                total = None
                for b in range(3):
                    for c in range(3):
                        part = exact(taps[b][c], (shift == 4 * b + c + parity).astype(jnp.bfloat16))
                        total = part if total is None else total + part
                total = total.astype(jnp.bfloat16)
                for a in range(3):
                    at = (2 - a) * 2 * C + parity * C + odd * C // 2
                    first_ref[pl.ds(at, C // 2), :] = total[a * C // 2 : (a + 1) * C // 2]


def swapped(block, axis, *others):
    count = lax.axis_size(axis)
    results = []
    for start in (1, 0):
        pairs = [(i, i + 1) for i in range(start, count - 1, 2)]
        if start == 0 and others:
            block = after(block, *others)
        results.append(lax.ppermute(block, axis, pairs + [(j, i) for i, j in pairs]))
    return results


def after(value, *others):
    return lax.optimization_barrier((value, *others))[0]


def in_vmem(value):
    return pltpu.with_memory_space_constraint(value, pltpu.VMEM)


def local(volume, conv_weight, down_weight):
    bands = lax.axis_size("filt")
    count, planes, all_rows, width = volume.shape
    band = all_rows // bands
    window = BELOW + band + ABOVE
    half = width // 2
    hid_rows = band + 1
    vmem = pl.BlockSpec(memory_space=pltpu.VMEM)
    params = pltpu.CompilerParams(vmem_limit_bytes=VMEM_LIMIT)
    cost = pl.CostEstimate(flops=1, transcendentals=0, bytes_accessed=1)
    direct = count == 16 and bands == 4
    distances = (0, 3, 1, 2) if direct else ()
    ranges = [(0, 48), (0, 16), (16, 32), (48, 16)] if direct else [(0, C)]
    lay = pl.pallas_call(
        functools.partial(weight_kernel, distances, ranges),
        out_shape=[pltpu.VMEM((C2, 28 * C), jnp.bfloat16)]
        + [pltpu.VMEM((6 * C, 12 * channels), jnp.bfloat16) for _, channels in ranges],
        in_specs=[vmem] * 2,
        out_specs=[vmem] * (1 + len(ranges)),
        compiler_params=params,
        cost_estimate=cost,
    )
    def convolve(feature, groups, second=None):
        arrays = [] if feature is None else [feature]
        last = second is not None
        arrays += [second] if last else []
        for _, *given in groups:
            arrays += given
        kinds = [group for group, *_ in groups]
        scratch = [pltpu.VMEM((hid_rows * 9 * C, half), jnp.bfloat16)] * last
        for group in kinds:
            slots = 2 if group.inside else 4
            scratch.append(pltpu.VMEM((slots, window * 4 * group.channels, half), jnp.bfloat16))
        if last:
            shape = pltpu.VMEM((band // 2, C2, half), jnp.bfloat16)
        else:
            shape = pltpu.VMEM((hid_rows * 6 * C, half), jnp.float32)
        return pl.pallas_call(
            functools.partial(conv_kernel, kinds, window, feature is None, last),
            out_shape=shape,
            in_specs=[vmem] * len(arrays),
            out_specs=vmem,
            scratch_shapes=scratch,
            compiler_params=params,
            cost_estimate=pl.CostEstimate(flops=1 << 33, transcendentals=0, bytes_accessed=1 << 24),
        )(*map(in_vmem, arrays))

    if direct:
        step = 16
        cut = (window + 1) // 2
        sends = [(d, 0, window) for d in distances[:3]] + [(2, 0, cut), (2, cut, window)]
        sent = pl.pallas_call(
            functools.partial(send_kernel, band, sends),
            out_shape=[
                jax.ShapeDtypeStruct((high - low, planes, count, width), jnp.bfloat16)
                for _, low, high in sends
            ],
            in_specs=[pl.BlockSpec(memory_space=pltpu.HBM)],
            out_specs=[vmem] * len(sends),
            scratch_shapes=[
                pltpu.VMEM((planes * all_rows // step, count, step, width), jnp.bfloat16),
                pltpu.VMEM((BELOW + all_rows + ABOVE, planes, count, width), jnp.bfloat16),
                pltpu.SemaphoreType.DMA((planes * all_rows // step,)),
            ],
            compiler_params=params,
            cost_estimate=cost,
        )(pltpu.with_memory_space_constraint(volume, pltpu.HBM))
        second, *firsts = lay(conv_weight, down_weight)
        own = []
        for (d, _, _), piece in zip(sends, sent):
            if d:
                piece = lax.ppermute(piece, "filt", [(i, i ^ d) for i in range(bands)])
            own.append(piece)
        mine = swapped(after(own[0], firsts[0]), "space")
        middle = pl.pallas_call(
            join_kernel,
            out_shape=pltpu.VMEM((2 * window, planes, count, width), jnp.bfloat16),
            in_specs=[vmem] * 2,
            out_specs=vmem,
            compiler_params=params,
            cost_estimate=cost,
        )(*map(in_vmem, own[1:3]))
        middles = swapped(middle, "space")
        all_three, of_own, of_middle, of_last = firsts
        full = (0, window)
        feature = convolve(
            None,
            [
                (
                    Group(True, 48, [(0, 0, 0, *full), (1, 0, 16, *full), (1, window, 32, *full)]),
                    all_three,
                    own[0],
                    middle,
                ),
                (Group(False, 16, [(0, 0, 0, *full), (1, 0, 0, *full)]), of_own, *mine),
            ],
        )
        heads = swapped(after(own[3], feature), "space")
        tails = swapped(after(own[4], feature), "space")
        middles = [after(block, own[4]) for block in middles]
        in_middle = [(i, at * window, at * 16, *full) for i in range(2) for at in range(2)]
        halves = ((0, cut), (cut, window))
        feature = convolve(
            feature,
            [
                (Group(True, 16, [(i, 0, 0, *halves[i]) for i in range(2)]), of_last, own[3], own[4]),
                (Group(False, 32, in_middle), of_middle, *middles),
            ],
        )
        in_last = [(i, 0, 0, *halves[i // 2]) for i in range(4)]
        coarse = convolve(feature, [(Group(False, 16, in_last), of_last, *heads, *tails)], second)
    else:
        field = jnp.transpose(volume, (2, 1, 0, 3))
        field = jnp.concatenate([field[..., ::2], field[..., 1::2]], axis=-1)
        field = jnp.pad(field, ((BELOW, ABOVE), (0, 0), (0, 0), (0, 0)))
        sent = jnp.stack([field[t * band : t * band + window] for t in range(bands)])
        got = lax.all_to_all(sent, "filt", split_axis=0, concat_axis=0, tiled=True)
        own = jnp.transpose(got, (1, 2, 0, 3, 4)).reshape(window, planes, C, width)
        second, *firsts = lay(conv_weight, down_weight)
        inside = (Group(True, C, [(0, 0, 0, 0, window)]), firsts[0], own)
        outside = (Group(False, C, [(0, 0, 0, 0, window), (1, 0, 0, 0, window)]), firsts[0], *swapped(own, "space"))
        coarse = convolve(None, [inside, outside], second)
    return jnp.transpose(coarse, (1, 0, 2))[:, None]


def solution(mesh):
    return jax.shard_map(
        local,
        mesh=mesh,
        in_specs=(P("filt", ("groups", "space"), None, None), P(), P()),
        out_specs=P(None, ("groups", "space"), "filt", None),
        check_vma=False,
    )
```

```python
import functools

import jax
import jax.numpy as jnp
from jax import lax
from jax.experimental import pallas as pl
from jax.experimental.pallas import tpu as pltpu
from jax.sharding import PartitionSpec as P

C = 64
C2 = 128
BELOW, ABOVE = 2, 1
negative_slope = 0.01
VMEM_LIMIT = 20 * 1024 * 1024


def split_matrix(width):
    half = width // 2
    source = lax.broadcasted_iota(jnp.int32, (width, width), 0)
    column = lax.broadcasted_iota(jnp.int32, (width, width), 1)
    wanted = jnp.where(column < half, 2 * column, 2 * (column - half) + 1)
    return jnp.where(source == wanted, 1.0, 0.0).astype(jnp.bfloat16)


def turn_matrix(count, rows):
    size = count * rows
    target = lax.broadcasted_iota(jnp.int32, (size, size), 0)
    source = lax.broadcasted_iota(jnp.int32, (size, size), 1)
    wanted = lax.rem(target, count) * rows + lax.div(target, count)
    return jnp.where(source == wanted, 1.0, 0.0).astype(jnp.bfloat16)


def send_kernel(band, parts, volume_ref, *refs):
    out_refs, (block_ref, field_ref, sems) = refs[:-3], refs[-3:]
    count, planes, all_rows, width = volume_ref.shape
    step = block_ref.shape[2]
    places = [(p, at) for at in range(0, all_rows, step) for p in range(planes)]
    copies = [
        pltpu.make_async_copy(volume_ref.at[:, p, pl.ds(at, step), :], block_ref.at[i], sems.at[i])
        for i, (p, at) in enumerate(places)
    ]
    for copy in copies:
        copy.start()
    turn = turn_matrix(count, step)
    field_ref[pl.ds(0, BELOW)] = jnp.zeros((BELOW, planes, count, width), jnp.bfloat16)
    field_ref[pl.ds(BELOW + all_rows, ABOVE)] = jnp.zeros((ABOVE, planes, count, width), jnp.bfloat16)
    for copy in copies:
        copy.wait()
    size = count * step
    wide = jnp.concatenate([block_ref[i].reshape(size, width) for i in range(len(places))], axis=1)
    wide = jnp.dot(turn, wide, preferred_element_type=jnp.float32).astype(jnp.bfloat16)
    tall = jnp.concatenate([wide[:, i * width // 2 : (i + 1) * width // 2] for i in range(2 * len(places))])
    tall = jnp.dot(tall, split_matrix(width // 2), preferred_element_type=jnp.float32).astype(jnp.bfloat16)
    cut = width // 4
    for i, (p, at) in enumerate(places):
        left, right = tall[2 * i * size : (2 * i + 1) * size], tall[(2 * i + 1) * size : (2 * i + 2) * size]
        block = jnp.concatenate([left[:, :cut], right[:, :cut], left[:, cut:], right[:, cut:]], axis=1)
        field_ref[pl.ds(BELOW + at, step), p] = block.reshape(step, count, width)
    me = lax.axis_index("filt")
    for (d, low, _), out_ref in zip(parts, out_refs):
        start = lax.bitwise_xor(me, d) * band + low
        out_ref[...] = field_ref[pl.ds(start, out_ref.shape[0])]


def store_taps(taps_ref, row, at, channels, cell):
    count, half = cell.shape[0], cell.shape[1] // 2
    lane = lax.broadcasted_iota(jnp.int32, (count, half), 1)
    even, odd = cell[:, :half], cell[:, half:]
    before = jnp.where(lane == 0, 0.0, pltpu.roll(odd.astype(jnp.float32), 1, 1))
    after_it = jnp.where(lane == half - 1, 0.0, pltpu.roll(even.astype(jnp.float32), half - 1, 1))
    for k, value in enumerate((before.astype(jnp.bfloat16), even, odd, after_it.astype(jnp.bfloat16))):
        taps_ref[pl.ds((4 * row + k) * channels + at, count), :] = value


def plane_parts(total, weight_ref, taps, y, p, depth):
    size = 2 * C
    z_low, z_high = max(0, p - 2), min(2, p)
    first = 2 - (p - z_low)
    weight = weight_ref[pl.ds(first * size, (z_high - z_low + 1) * size), :]
    part = jnp.dot(weight, taps[pl.ds(y * depth, 3 * depth), :], preferred_element_type=jnp.float32)
    for z in range(z_low, z_high + 1):
        piece = part[(z - z_low) * size : (z - z_low + 1) * size]
        total[z] = piece if total[z] is None else total[z] + piece


def join_kernel(one_ref, two_ref, out_ref):
    rows = one_ref.shape[0]
    out_ref[:rows] = one_ref[...]
    out_ref[rows:] = two_ref[...]


class Group:
    def __init__(self, inside, channels, blocks):
        self.inside, self.channels, self.blocks = inside, channels, blocks
        self.planes = (2, 3) if inside else (0, 1, 4)
        self.arrays = 1 + max(block[0] for block in blocks)


def conv_kernel(groups, window, first, last, *refs):
    space, band = lax.axis_index("space"), lax.axis_index("filt")
    odd = lax.rem(space, 2)
    places = ((2 * odd, 1 + 2 * odd), (2 - 2 * odd, 3 - 2 * odd))
    refs = list(refs)
    feature_ref = None if first else refs.pop(0)
    second_ref = refs.pop(0) if last else None
    inputs = [[refs.pop(0) for _ in range(1 + group.arrays)] for group in groups]
    out_ref = refs.pop(0)
    hid_ref = refs.pop(0) if last else None
    half = out_ref.shape[-1]
    for group, (_, *blocks), taps_ref in zip(groups, inputs, refs):
        for i, row, at, low, high in group.blocks:
            for r in range(low, high):
                for k in range(2):
                    place = k if group.inside else places[i % 2][k]
                    store_taps(taps_ref.at[place], r, at, group.channels, blocks[i][row + r - low, k])
    size = 2 * C
    lane = lax.broadcasted_iota(jnp.int32, (C, half), 1)
    for y in range(window - 2):
        total = [None if first else feature_ref[pl.ds((y * 3 + z) * size, size), :] for z in range(3)]
        for group, (weight_ref, *_), taps_ref in zip(groups, inputs, refs):
            for k, p in enumerate(group.planes):
                plane_parts(total, weight_ref, taps_ref.at[k], y, p, 4 * group.channels)
        for z in range(3):
            if not last:
                out_ref[pl.ds((y * 3 + z) * size, size), :] = total[z]
                continue
            value = total[z]
            value = jnp.where(value > 0, value, negative_slope * value)
            if z == 0:
                value = jnp.where(space > 0, value, 0.0)
            if y == 0:
                value = jnp.where(band > 0, value, 0.0)
            value = value.astype(jnp.bfloat16)
            before = jnp.where(lane == 0, 0.0, pltpu.roll(value[C:].astype(jnp.float32), 1, 1))
            base = (y * 3 + z) * 3 * C
            hid_ref[pl.ds(base, C), :] = before.astype(jnp.bfloat16)
            hid_ref[pl.ds(base + C, 2 * C), :] = value
    if last:
        for y in range(out_ref.shape[0]):
            out_ref[y] = jnp.dot(
                second_ref[:, : 27 * C],
                hid_ref[pl.ds(2 * y * 9 * C, 27 * C), :],
                preferred_element_type=jnp.float32,
            ).astype(jnp.bfloat16)


def exact(left, right):
    return jnp.dot(left, right, preferred_element_type=jnp.float32)


def weight_kernel(distances, ranges, conv_ref, down_ref, second_ref, *first_refs):
    row = lax.broadcasted_iota(jnp.int32, (2 * C, 2 * C), 0)
    lane = lax.broadcasted_iota(jnp.int32, (2 * C, 2 * C), 1)
    hidden = 2 * lax.rem(lane, C // 2) + lax.div(lax.rem(lane, C), C // 2)
    pair = [
        [((row == C * odd + hidden) & (lax.div(lane, C) == k)).astype(jnp.bfloat16) for k in range(2)]
        for odd in range(2)
    ]
    in_order = (row == 2 * lax.rem(lane, C) + lax.div(lane, C)).astype(jnp.bfloat16)
    down = [[down_ref[a, b].reshape(3, C, 2 * C) for b in range(3)] for a in range(3)]
    for j in range(14):
        halves = []
        for odd in range(2):
            total = None
            for k in range(2):
                t = 2 * j + k
                if t < 27:
                    part = exact(down[t // 3 % 3][t // 9][t % 3], pair[odd][k])
                    total = part if total is None else total + part
            halves.append(total.astype(jnp.bfloat16))
        second_ref[:, pl.ds(2 * C * j, 2 * C)] = exact(in_order, jnp.concatenate(halves)).astype(jnp.bfloat16)
    conv = [[conv_ref[a, b].reshape(3, C // 2, 2 * C) for b in range(3)] for a in range(3)]
    taps = [[jnp.concatenate([conv[a][b][c] for a in range(3)]) for c in range(3)] for b in range(3)]
    for (start, channels), first_ref in zip(ranges, first_refs):
        row = lax.broadcasted_iota(jnp.int32, (2 * C, 12 * channels), 0)
        lane = lax.broadcasted_iota(jnp.int32, (2 * C, 12 * channels), 1)
        place = start + lax.rem(lane, channels)
        source = place
        if distances:
            me, count = lax.axis_index("filt"), C // len(distances)
            for i, d in enumerate(distances):
                moved = lax.bitwise_xor(me, d) * count + place - i * count
                source = jnp.where(lax.div(place, count) == i, moved, source)
        for odd in range(2):
            shift = jnp.where(row == C * odd + source, lax.div(lane, channels), -1)
            for parity in range(2):
                total = None
                for b in range(3):
                    for c in range(3):
                        part = exact(taps[b][c], (shift == 4 * b + c + parity).astype(jnp.bfloat16))
                        total = part if total is None else total + part
                total = total.astype(jnp.bfloat16)
                for a in range(3):
                    at = (2 - a) * 2 * C + parity * C + odd * C // 2
                    first_ref[pl.ds(at, C // 2), :] = total[a * C // 2 : (a + 1) * C // 2]


def swapped(block, axis, *others):
    count = lax.axis_size(axis)
    results = []
    for start in (1, 0):
        pairs = [(i, i + 1) for i in range(start, count - 1, 2)]
        if start == 0 and others:
            block = after(block, *others)
        results.append(lax.ppermute(block, axis, pairs + [(j, i) for i, j in pairs]))
    return results


def after(value, *others):
    return lax.optimization_barrier((value, *others))[0]


def in_vmem(value):
    return pltpu.with_memory_space_constraint(value, pltpu.VMEM)


def local(volume, conv_weight, down_weight):
    bands = lax.axis_size("filt")
    count, planes, all_rows, width = volume.shape
    band = all_rows // bands
    window = BELOW + band + ABOVE
    half = width // 2
    hid_rows = band + 1
    vmem = pl.BlockSpec(memory_space=pltpu.VMEM)
    params = pltpu.CompilerParams(vmem_limit_bytes=VMEM_LIMIT)
    cost = pl.CostEstimate(flops=1, transcendentals=0, bytes_accessed=1)
    direct = count == 16 and bands == 4
    distances = (0, 2, 1, 3) if direct else ()
    ranges = [(0, 48), (0, 16), (16, 32), (48, 16)] if direct else [(0, C)]
    lay = pl.pallas_call(
        functools.partial(weight_kernel, distances, ranges),
        out_shape=[pltpu.VMEM((C2, 28 * C), jnp.bfloat16)]
        + [pltpu.VMEM((6 * C, 12 * channels), jnp.bfloat16) for _, channels in ranges],
        in_specs=[vmem] * 2,
        out_specs=[vmem] * (1 + len(ranges)),
        compiler_params=params,
        cost_estimate=cost,
    )
    def convolve(feature, groups, second=None):
        arrays = [] if feature is None else [feature]
        last = second is not None
        arrays += [second] if last else []
        for _, *given in groups:
            arrays += given
        kinds = [group for group, *_ in groups]
        scratch = [pltpu.VMEM((hid_rows * 9 * C, half), jnp.bfloat16)] * last
        for group in kinds:
            slots = 2 if group.inside else 4
            scratch.append(pltpu.VMEM((slots, window * 4 * group.channels, half), jnp.bfloat16))
        if last:
            shape = pltpu.VMEM((band // 2, C2, half), jnp.bfloat16)
        else:
            shape = pltpu.VMEM((hid_rows * 6 * C, half), jnp.float32)
        return pl.pallas_call(
            functools.partial(conv_kernel, kinds, window, feature is None, last),
            out_shape=shape,
            in_specs=[vmem] * len(arrays),
            out_specs=vmem,
            scratch_shapes=scratch,
            compiler_params=params,
            cost_estimate=pl.CostEstimate(flops=1 << 33, transcendentals=0, bytes_accessed=1 << 24),
        )(*map(in_vmem, arrays))

    if direct:
        step = 16
        cut = (window + 1) // 2
        sends = [(d, 0, window) for d in distances[:3]] + [(distances[3], 0, cut), (distances[3], cut, window)]
        sent = pl.pallas_call(
            functools.partial(send_kernel, band, sends),
            out_shape=[
                jax.ShapeDtypeStruct((high - low, planes, count, width), jnp.bfloat16)
                for _, low, high in sends
            ],
            in_specs=[pl.BlockSpec(memory_space=pltpu.HBM)],
            out_specs=[vmem] * len(sends),
            scratch_shapes=[
                pltpu.VMEM((planes * all_rows // step, count, step, width), jnp.bfloat16),
                pltpu.VMEM((BELOW + all_rows + ABOVE, planes, count, width), jnp.bfloat16),
                pltpu.SemaphoreType.DMA((planes * all_rows // step,)),
            ],
            compiler_params=params,
            cost_estimate=cost,
        )(pltpu.with_memory_space_constraint(volume, pltpu.HBM))
        second, *firsts = lay(conv_weight, down_weight)
        own = []
        for (d, _, _), piece in zip(sends, sent):
            if d:
                piece = lax.ppermute(piece, "filt", [(i, i ^ d) for i in range(bands)])
            own.append(piece)
        mine = swapped(after(own[0], firsts[0]), "space")
        middle = pl.pallas_call(
            join_kernel,
            out_shape=pltpu.VMEM((2 * window, planes, count, width), jnp.bfloat16),
            in_specs=[vmem] * 2,
            out_specs=vmem,
            compiler_params=params,
            cost_estimate=cost,
        )(*map(in_vmem, own[1:3]))
        middles = swapped(middle, "space")
        all_three, of_own, of_middle, of_last = firsts
        full = (0, window)
        feature = convolve(
            None,
            [
                (
                    Group(True, 48, [(0, 0, 0, *full), (1, 0, 16, *full), (1, window, 32, *full)]),
                    all_three,
                    own[0],
                    middle,
                ),
                (Group(False, 16, [(0, 0, 0, *full), (1, 0, 0, *full)]), of_own, *mine),
            ],
        )
        heads = swapped(after(own[3], feature), "space")
        tails = swapped(after(own[4], feature), "space")
        middles = [after(block, own[4]) for block in middles]
        in_middle = [(i, at * window, at * 16, *full) for i in range(2) for at in range(2)]
        halves = ((0, cut), (cut, window))
        feature = convolve(
            feature,
            [
                (Group(True, 16, [(i, 0, 0, *halves[i]) for i in range(2)]), of_last, own[3], own[4]),
                (Group(False, 32, in_middle), of_middle, *middles),
            ],
        )
        in_last = [(i, 0, 0, *halves[i // 2]) for i in range(4)]
        coarse = convolve(feature, [(Group(False, 16, in_last), of_last, *heads, *tails)], second)
    else:
        field = jnp.transpose(volume, (2, 1, 0, 3))
        field = jnp.concatenate([field[..., ::2], field[..., 1::2]], axis=-1)
        field = jnp.pad(field, ((BELOW, ABOVE), (0, 0), (0, 0), (0, 0)))
        sent = jnp.stack([field[t * band : t * band + window] for t in range(bands)])
        got = lax.all_to_all(sent, "filt", split_axis=0, concat_axis=0, tiled=True)
        own = jnp.transpose(got, (1, 2, 0, 3, 4)).reshape(window, planes, C, width)
        second, *firsts = lay(conv_weight, down_weight)
        inside = (Group(True, C, [(0, 0, 0, 0, window)]), firsts[0], own)
        outside = (Group(False, C, [(0, 0, 0, 0, window), (1, 0, 0, 0, window)]), firsts[0], *swapped(own, "space"))
        coarse = convolve(None, [inside, outside], second)
    return jnp.transpose(coarse, (1, 0, 2))[:, None]


def solution(mesh):
    return jax.shard_map(
        local,
        mesh=mesh,
        in_specs=(P("filt", ("groups", "space"), None, None), P(), P()),
        out_specs=P(None, ("groups", "space"), "filt", None),
        check_vma=False,
    )
```

```python
import functools

import jax
import jax.numpy as jnp
from jax import lax
from jax.experimental import pallas as pl
from jax.experimental.pallas import tpu as pltpu
from jax.sharding import PartitionSpec as P

C = 64
C2 = 128
BELOW, ABOVE = 2, 1
negative_slope = 0.01
VMEM_LIMIT = 20 * 1024 * 1024


def split_matrix(width):
    half = width // 2
    source = lax.broadcasted_iota(jnp.int32, (width, width), 0)
    column = lax.broadcasted_iota(jnp.int32, (width, width), 1)
    wanted = jnp.where(column < half, 2 * column, 2 * (column - half) + 1)
    return jnp.where(source == wanted, 1.0, 0.0).astype(jnp.bfloat16)


def turn_matrix(count, rows):
    size = count * rows
    target = lax.broadcasted_iota(jnp.int32, (size, size), 0)
    source = lax.broadcasted_iota(jnp.int32, (size, size), 1)
    wanted = lax.rem(target, count) * rows + lax.div(target, count)
    return jnp.where(source == wanted, 1.0, 0.0).astype(jnp.bfloat16)


def send_kernel(band, parts, volume_ref, *refs):
    out_refs, (block_ref, field_ref, sems) = refs[:-3], refs[-3:]
    count, planes, all_rows, width = volume_ref.shape
    step = block_ref.shape[2]
    places = [(p, at) for at in range(0, all_rows, step) for p in range(planes)]
    copies = [
        pltpu.make_async_copy(volume_ref.at[:, p, pl.ds(at, step), :], block_ref.at[i], sems.at[i])
        for i, (p, at) in enumerate(places)
    ]
    for copy in copies:
        copy.start()
    turn = turn_matrix(count, step)
    field_ref[pl.ds(0, BELOW)] = jnp.zeros((BELOW, planes, count, width), jnp.bfloat16)
    field_ref[pl.ds(BELOW + all_rows, ABOVE)] = jnp.zeros((ABOVE, planes, count, width), jnp.bfloat16)
    for copy in copies:
        copy.wait()
    size = count * step
    wide = jnp.concatenate([block_ref[i].reshape(size, width) for i in range(len(places))], axis=1)
    wide = jnp.dot(turn, wide, preferred_element_type=jnp.float32).astype(jnp.bfloat16)
    tall = jnp.concatenate([wide[:, i * width // 2 : (i + 1) * width // 2] for i in range(2 * len(places))])
    tall = jnp.dot(tall, split_matrix(width // 2), preferred_element_type=jnp.float32).astype(jnp.bfloat16)
    cut = width // 4
    for i, (p, at) in enumerate(places):
        left, right = tall[2 * i * size : (2 * i + 1) * size], tall[(2 * i + 1) * size : (2 * i + 2) * size]
        block = jnp.concatenate([left[:, :cut], right[:, :cut], left[:, cut:], right[:, cut:]], axis=1)
        field_ref[pl.ds(BELOW + at, step), p] = block.reshape(step, count, width)
    me = lax.axis_index("filt")
    for (d, low, _), out_ref in zip(parts, out_refs):
        start = lax.bitwise_xor(me, d) * band + low
        out_ref[...] = field_ref[pl.ds(start, out_ref.shape[0])]


def store_taps(taps_ref, row, at, channels, cell):
    count, half = cell.shape[0], cell.shape[1] // 2
    lane = lax.broadcasted_iota(jnp.int32, (count, half), 1)
    even, odd = cell[:, :half], cell[:, half:]
    before = jnp.where(lane == 0, 0.0, pltpu.roll(odd.astype(jnp.float32), 1, 1))
    after_it = jnp.where(lane == half - 1, 0.0, pltpu.roll(even.astype(jnp.float32), half - 1, 1))
    for k, value in enumerate((before.astype(jnp.bfloat16), even, odd, after_it.astype(jnp.bfloat16))):
        taps_ref[pl.ds((4 * row + k) * channels + at, count), :] = value


def plane_parts(total, weight_ref, taps, y, p, depth):
    size = 2 * C
    z_low, z_high = max(0, p - 2), min(2, p)
    first = 2 - (p - z_low)
    weight = weight_ref[pl.ds(first * size, (z_high - z_low + 1) * size), :]
    part = jnp.dot(weight, taps[pl.ds(y * depth, 3 * depth), :], preferred_element_type=jnp.float32)
    for z in range(z_low, z_high + 1):
        piece = part[(z - z_low) * size : (z - z_low + 1) * size]
        total[z] = piece if total[z] is None else total[z] + piece


def join_kernel(one_ref, two_ref, out_ref):
    rows = one_ref.shape[0]
    out_ref[:rows] = one_ref[...]
    out_ref[rows:] = two_ref[...]


class Group:
    def __init__(self, inside, channels, blocks):
        self.inside, self.channels, self.blocks = inside, channels, blocks
        self.planes = (2, 3) if inside else (0, 1, 4)
        self.arrays = 1 + max(block[0] for block in blocks)


def conv_kernel(groups, window, first, last, *refs):
    space, band = lax.axis_index("space"), lax.axis_index("filt")
    odd = lax.rem(space, 2)
    places = ((2 * odd, 1 + 2 * odd), (2 - 2 * odd, 3 - 2 * odd))
    refs = list(refs)
    feature_ref = None if first else refs.pop(0)
    second_ref = refs.pop(0) if last else None
    inputs = [[refs.pop(0) for _ in range(1 + group.arrays)] for group in groups]
    out_ref = refs.pop(0)
    hid_ref = refs.pop(0) if last else None
    half = out_ref.shape[-1]
    for group, (_, *blocks), taps_ref in zip(groups, inputs, refs):
        for i, row, at, low, high in group.blocks:
            for r in range(low, high):
                for k in range(2):
                    place = k if group.inside else places[i % 2][k]
                    store_taps(taps_ref.at[place], r, at, group.channels, blocks[i][row + r - low, k])
    size = 2 * C
    lane = lax.broadcasted_iota(jnp.int32, (C, half), 1)
    for y in range(window - 2):
        total = [None if first else feature_ref[pl.ds((y * 3 + z) * size, size), :] for z in range(3)]
        for group, (weight_ref, *_), taps_ref in zip(groups, inputs, refs):
            for k, p in enumerate(group.planes):
                plane_parts(total, weight_ref, taps_ref.at[k], y, p, 4 * group.channels)
        for z in range(3):
            if not last:
                out_ref[pl.ds((y * 3 + z) * size, size), :] = total[z]
                continue
            value = total[z]
            value = jnp.where(value > 0, value, negative_slope * value)
            if z == 0:
                value = jnp.where(space > 0, value, 0.0)
            if y == 0:
                value = jnp.where(band > 0, value, 0.0)
            value = value.astype(jnp.bfloat16)
            before = jnp.where(lane == 0, 0.0, pltpu.roll(value[C:].astype(jnp.float32), 1, 1))
            base = (y * 3 + z) * 3 * C
            hid_ref[pl.ds(base, C), :] = before.astype(jnp.bfloat16)
            hid_ref[pl.ds(base + C, 2 * C), :] = value
    if last:
        for y in range(out_ref.shape[0]):
            out_ref[y] = jnp.dot(
                second_ref[:, : 27 * C],
                hid_ref[pl.ds(2 * y * 9 * C, 27 * C), :],
                preferred_element_type=jnp.float32,
            ).astype(jnp.bfloat16)


def exact(left, right):
    return jnp.dot(left, right, preferred_element_type=jnp.float32)


def weight_kernel(distances, ranges, conv_ref, down_ref, second_ref, *first_refs):
    row = lax.broadcasted_iota(jnp.int32, (2 * C, 2 * C), 0)
    lane = lax.broadcasted_iota(jnp.int32, (2 * C, 2 * C), 1)
    hidden = 2 * lax.rem(lane, C // 2) + lax.div(lax.rem(lane, C), C // 2)
    pair = [
        [((row == C * odd + hidden) & (lax.div(lane, C) == k)).astype(jnp.bfloat16) for k in range(2)]
        for odd in range(2)
    ]
    in_order = (row == 2 * lax.rem(lane, C) + lax.div(lane, C)).astype(jnp.bfloat16)
    down = [[down_ref[a, b].reshape(3, C, 2 * C) for b in range(3)] for a in range(3)]
    for j in range(14):
        halves = []
        for odd in range(2):
            total = None
            for k in range(2):
                t = 2 * j + k
                if t < 27:
                    part = exact(down[t // 3 % 3][t // 9][t % 3], pair[odd][k])
                    total = part if total is None else total + part
            halves.append(total.astype(jnp.bfloat16))
        second_ref[:, pl.ds(2 * C * j, 2 * C)] = exact(in_order, jnp.concatenate(halves)).astype(jnp.bfloat16)
    conv = [[conv_ref[a, b].reshape(3, C // 2, 2 * C) for b in range(3)] for a in range(3)]
    taps = [[jnp.concatenate([conv[a][b][c] for a in range(3)]) for c in range(3)] for b in range(3)]
    for (start, channels), first_ref in zip(ranges, first_refs):
        row = lax.broadcasted_iota(jnp.int32, (2 * C, 12 * channels), 0)
        lane = lax.broadcasted_iota(jnp.int32, (2 * C, 12 * channels), 1)
        place = start + lax.rem(lane, channels)
        source = place
        if distances:
            me, count = lax.axis_index("filt"), C // len(distances)
            for i, d in enumerate(distances):
                moved = lax.bitwise_xor(me, d) * count + place - i * count
                source = jnp.where(lax.div(place, count) == i, moved, source)
        for odd in range(2):
            shift = jnp.where(row == C * odd + source, lax.div(lane, channels), -1)
            for parity in range(2):
                total = None
                for b in range(3):
                    for c in range(3):
                        part = exact(taps[b][c], (shift == 4 * b + c + parity).astype(jnp.bfloat16))
                        total = part if total is None else total + part
                total = total.astype(jnp.bfloat16)
                for a in range(3):
                    at = (2 - a) * 2 * C + parity * C + odd * C // 2
                    first_ref[pl.ds(at, C // 2), :] = total[a * C // 2 : (a + 1) * C // 2]


def swapped(block, axis, *others):
    count = lax.axis_size(axis)
    results = []
    for start in (1, 0):
        pairs = [(i, i + 1) for i in range(start, count - 1, 2)]
        if start == 0 and others:
            block = after(block, *others)
        results.append(lax.ppermute(block, axis, pairs + [(j, i) for i, j in pairs]))
    return results


def after(value, *others):
    return lax.optimization_barrier((value, *others))[0]


def in_vmem(value):
    return pltpu.with_memory_space_constraint(value, pltpu.VMEM)


def local(volume, conv_weight, down_weight):
    bands = lax.axis_size("filt")
    count, planes, all_rows, width = volume.shape
    band = all_rows // bands
    window = BELOW + band + ABOVE
    half = width // 2
    hid_rows = band + 1
    vmem = pl.BlockSpec(memory_space=pltpu.VMEM)
    params = pltpu.CompilerParams(vmem_limit_bytes=VMEM_LIMIT)
    cost = pl.CostEstimate(flops=1, transcendentals=0, bytes_accessed=1)
    direct = count == 16 and bands == 4
    distances = (0, 2, 1, 3) if direct else ()
    ranges = [(0, 48), (0, 16), (16, 32), (48, 16)] if direct else [(0, C)]
    lay = pl.pallas_call(
        functools.partial(weight_kernel, distances, ranges),
        out_shape=[pltpu.VMEM((C2, 28 * C), jnp.bfloat16)]
        + [pltpu.VMEM((6 * C, 12 * channels), jnp.bfloat16) for _, channels in ranges],
        in_specs=[vmem] * 2,
        out_specs=[vmem] * (1 + len(ranges)),
        compiler_params=params,
        cost_estimate=cost,
    )
    def convolve(feature, groups, second=None):
        arrays = [] if feature is None else [feature]
        last = second is not None
        arrays += [second] if last else []
        for _, *given in groups:
            arrays += given
        kinds = [group for group, *_ in groups]
        scratch = [pltpu.VMEM((hid_rows * 9 * C, half), jnp.bfloat16)] * last
        for group in kinds:
            slots = 2 if group.inside else 4
            scratch.append(pltpu.VMEM((slots, window * 4 * group.channels, half), jnp.bfloat16))
        if last:
            shape = pltpu.VMEM((band // 2, C2, half), jnp.bfloat16)
        else:
            shape = pltpu.VMEM((hid_rows * 6 * C, half), jnp.float32)
        return pl.pallas_call(
            functools.partial(conv_kernel, kinds, window, feature is None, last),
            out_shape=shape,
            in_specs=[vmem] * len(arrays),
            out_specs=vmem,
            scratch_shapes=scratch,
            compiler_params=params,
            cost_estimate=pl.CostEstimate(flops=1 << 33, transcendentals=0, bytes_accessed=1 << 24),
        )(*map(in_vmem, arrays))

    if direct:
        step = 16
        cut = (window + 1) // 2
        sends = [(d, 0, window) for d in distances[:3]] + [(distances[3], 0, cut), (distances[3], cut, window)]
        sent = pl.pallas_call(
            functools.partial(send_kernel, band, sends),
            out_shape=[
                jax.ShapeDtypeStruct((high - low, planes, count, width), jnp.bfloat16)
                for _, low, high in sends
            ],
            in_specs=[pl.BlockSpec(memory_space=pltpu.HBM)],
            out_specs=[vmem] * len(sends),
            scratch_shapes=[
                pltpu.VMEM((planes * all_rows // step, count, step, width), jnp.bfloat16),
                pltpu.VMEM((BELOW + all_rows + ABOVE, planes, count, width), jnp.bfloat16),
                pltpu.SemaphoreType.DMA((planes * all_rows // step,)),
            ],
            compiler_params=params,
            cost_estimate=cost,
        )(pltpu.with_memory_space_constraint(volume, pltpu.HBM))
        second, *firsts = lay(
            pltpu.with_memory_space_constraint(conv_weight, pltpu.HBM),
            pltpu.with_memory_space_constraint(down_weight, pltpu.HBM),
        )
        own = []
        for (d, _, _), piece in zip(sends, sent):
            if d:
                piece = lax.ppermute(piece, "filt", [(i, i ^ d) for i in range(bands)])
            own.append(piece)
        mine = swapped(after(own[0], firsts[0]), "space")
        middle = pl.pallas_call(
            join_kernel,
            out_shape=pltpu.VMEM((2 * window, planes, count, width), jnp.bfloat16),
            in_specs=[vmem] * 2,
            out_specs=vmem,
            compiler_params=params,
            cost_estimate=cost,
        )(*map(in_vmem, own[1:3]))
        middles = swapped(middle, "space")
        all_three, of_own, of_middle, of_last = firsts
        full = (0, window)
        feature = convolve(
            None,
            [
                (
                    Group(True, 48, [(0, 0, 0, *full), (1, 0, 16, *full), (1, window, 32, *full)]),
                    all_three,
                    own[0],
                    middle,
                ),
                (Group(False, 16, [(0, 0, 0, *full), (1, 0, 0, *full)]), of_own, *mine),
            ],
        )
        heads = swapped(after(own[3], feature), "space")
        tails = swapped(after(own[4], feature), "space")
        middles = [after(block, own[4]) for block in middles]
        in_middle = [(i, at * window, at * 16, *full) for i in range(2) for at in range(2)]
        halves = ((0, cut), (cut, window))
        feature = convolve(
            feature,
            [
                (Group(True, 16, [(i, 0, 0, *halves[i]) for i in range(2)]), of_last, own[3], own[4]),
                (Group(False, 32, in_middle), of_middle, *middles),
            ],
        )
        in_last = [(i, 0, 0, *halves[i // 2]) for i in range(4)]
        coarse = convolve(feature, [(Group(False, 16, in_last), of_last, *heads, *tails)], second)
    else:
        field = jnp.transpose(volume, (2, 1, 0, 3))
        field = jnp.concatenate([field[..., ::2], field[..., 1::2]], axis=-1)
        field = jnp.pad(field, ((BELOW, ABOVE), (0, 0), (0, 0), (0, 0)))
        sent = jnp.stack([field[t * band : t * band + window] for t in range(bands)])
        got = lax.all_to_all(sent, "filt", split_axis=0, concat_axis=0, tiled=True)
        own = jnp.transpose(got, (1, 2, 0, 3, 4)).reshape(window, planes, C, width)
        second, *firsts = lay(conv_weight, down_weight)
        inside = (Group(True, C, [(0, 0, 0, 0, window)]), firsts[0], own)
        outside = (Group(False, C, [(0, 0, 0, 0, window), (1, 0, 0, 0, window)]), firsts[0], *swapped(own, "space"))
        coarse = convolve(None, [inside, outside], second)
    return jnp.transpose(coarse, (1, 0, 2))[:, None]


def solution(mesh):
    return jax.shard_map(
        local,
        mesh=mesh,
        in_specs=(P("filt", ("groups", "space"), None, None), P(), P()),
        out_specs=P(None, ("groups", "space"), "filt", None),
        check_vma=False,
    )
```

```python
import functools

import jax
import jax.numpy as jnp
from jax import lax
from jax.experimental import pallas as pl
from jax.experimental.pallas import tpu as pltpu
from jax.sharding import PartitionSpec as P

C = 64
C2 = 128
BELOW, ABOVE = 2, 1
negative_slope = 0.01
VMEM_LIMIT = 20 * 1024 * 1024


def split_matrix(width):
    half = width // 2
    source = lax.broadcasted_iota(jnp.int32, (width, width), 0)
    column = lax.broadcasted_iota(jnp.int32, (width, width), 1)
    wanted = jnp.where(column < half, 2 * column, 2 * (column - half) + 1)
    return jnp.where(source == wanted, 1.0, 0.0).astype(jnp.bfloat16)


def turn_matrix(count, rows):
    size = count * rows
    target = lax.broadcasted_iota(jnp.int32, (size, size), 0)
    source = lax.broadcasted_iota(jnp.int32, (size, size), 1)
    wanted = lax.rem(target, count) * rows + lax.div(target, count)
    return jnp.where(source == wanted, 1.0, 0.0).astype(jnp.bfloat16)


def send_kernel(band, parts, volume_ref, *refs):
    out_refs, (block_ref, field_ref, sems) = refs[:-3], refs[-3:]
    count, planes, all_rows, width = volume_ref.shape
    step = block_ref.shape[2]
    places = [(p, at) for at in range(0, all_rows, step) for p in range(planes)]
    copies = [
        pltpu.make_async_copy(volume_ref.at[:, p, pl.ds(at, step), :], block_ref.at[i], sems.at[i])
        for i, (p, at) in enumerate(places)
    ]
    for copy in copies:
        copy.start()
    turn = turn_matrix(count, step)
    field_ref[pl.ds(0, BELOW)] = jnp.zeros((BELOW, planes, count, width), jnp.bfloat16)
    field_ref[pl.ds(BELOW + all_rows, ABOVE)] = jnp.zeros((ABOVE, planes, count, width), jnp.bfloat16)
    for copy in copies:
        copy.wait()
    size = count * step
    wide = jnp.concatenate([block_ref[i].reshape(size, width) for i in range(len(places))], axis=1)
    wide = jnp.dot(turn, wide, preferred_element_type=jnp.float32).astype(jnp.bfloat16)
    tall = jnp.concatenate([wide[:, i * width // 2 : (i + 1) * width // 2] for i in range(2 * len(places))])
    tall = jnp.dot(tall, split_matrix(width // 2), preferred_element_type=jnp.float32).astype(jnp.bfloat16)
    cut = width // 4
    for i, (p, at) in enumerate(places):
        left, right = tall[2 * i * size : (2 * i + 1) * size], tall[(2 * i + 1) * size : (2 * i + 2) * size]
        block = jnp.concatenate([left[:, :cut], right[:, :cut], left[:, cut:], right[:, cut:]], axis=1)
        field_ref[pl.ds(BELOW + at, step), p] = block.reshape(step, count, width)
    me = lax.axis_index("filt")
    for (d, low, _), out_ref in zip(parts, out_refs):
        start = lax.bitwise_xor(me, d) * band + low
        out_ref[...] = field_ref[pl.ds(start, out_ref.shape[0])]


def store_taps(taps_ref, row, at, channels, cell):
    count, half = cell.shape[0], cell.shape[1] // 2
    lane = lax.broadcasted_iota(jnp.int32, (count, half), 1)
    even, odd = cell[:, :half], cell[:, half:]
    before = jnp.where(lane == 0, 0.0, pltpu.roll(odd.astype(jnp.float32), 1, 1))
    after_it = jnp.where(lane == half - 1, 0.0, pltpu.roll(even.astype(jnp.float32), half - 1, 1))
    for k, value in enumerate((before.astype(jnp.bfloat16), even, odd, after_it.astype(jnp.bfloat16))):
        taps_ref[pl.ds((4 * row + k) * channels + at, count), :] = value


def plane_parts(total, weight_ref, taps, y, p, depth):
    size = 2 * C
    z_low, z_high = max(0, p - 2), min(2, p)
    first = 2 - (p - z_low)
    weight = weight_ref[pl.ds(first * size, (z_high - z_low + 1) * size), :]
    part = jnp.dot(weight, taps[pl.ds(y * depth, 3 * depth), :], preferred_element_type=jnp.float32)
    for z in range(z_low, z_high + 1):
        piece = part[(z - z_low) * size : (z - z_low + 1) * size]
        total[z] = piece if total[z] is None else total[z] + piece


def join_kernel(one_ref, two_ref, out_ref):
    rows = one_ref.shape[0]
    out_ref[:rows] = one_ref[...]
    out_ref[rows:] = two_ref[...]


class Group:
    def __init__(self, inside, channels, blocks):
        self.inside, self.channels, self.blocks = inside, channels, blocks
        self.planes = (2, 3) if inside else (0, 1, 4)
        self.arrays = 1 + max(block[0] for block in blocks)


def conv_kernel(groups, window, first, last, *refs):
    space, band = lax.axis_index("space"), lax.axis_index("filt")
    odd = lax.rem(space, 2)
    places = ((2 * odd, 1 + 2 * odd), (2 - 2 * odd, 3 - 2 * odd))
    refs = list(refs)
    feature_ref = None if first else refs.pop(0)
    second_ref = refs.pop(0) if last else None
    inputs = [[refs.pop(0) for _ in range(1 + group.arrays)] for group in groups]
    out_ref = refs.pop(0)
    hid_ref = refs.pop(0) if last else None
    half = out_ref.shape[-1]
    for group, (_, *blocks), taps_ref in zip(groups, inputs, refs):
        for i, row, at, low, high in group.blocks:
            for r in range(low, high):
                for k in range(2):
                    place = k if group.inside else places[i % 2][k]
                    store_taps(taps_ref.at[place], r, at, group.channels, blocks[i][row + r - low, k])
    size = 2 * C
    lane = lax.broadcasted_iota(jnp.int32, (C, half), 1)
    for y in range(window - 2):
        total = [None if first else feature_ref[pl.ds((y * 3 + z) * size, size), :] for z in range(3)]
        for group, (weight_ref, *_), taps_ref in zip(groups, inputs, refs):
            for k, p in enumerate(group.planes):
                plane_parts(total, weight_ref, taps_ref.at[k], y, p, 4 * group.channels)
        for z in range(3):
            if not last:
                out_ref[pl.ds((y * 3 + z) * size, size), :] = total[z]
                continue
            value = total[z]
            value = jnp.where(value > 0, value, negative_slope * value)
            if z == 0:
                value = jnp.where(space > 0, value, 0.0)
            if y == 0:
                value = jnp.where(band > 0, value, 0.0)
            value = value.astype(jnp.bfloat16)
            before = jnp.where(lane == 0, 0.0, pltpu.roll(value[C:].astype(jnp.float32), 1, 1))
            base = (y * 3 + z) * 3 * C
            hid_ref[pl.ds(base, C), :] = before.astype(jnp.bfloat16)
            hid_ref[pl.ds(base + C, 2 * C), :] = value
    if last:
        for y in range(out_ref.shape[0]):
            out_ref[y] = jnp.dot(
                second_ref[:, : 27 * C],
                hid_ref[pl.ds(2 * y * 9 * C, 27 * C), :],
                preferred_element_type=jnp.float32,
            ).astype(jnp.bfloat16)


def exact(left, right):
    return jnp.dot(left, right, preferred_element_type=jnp.float32)


def weight_kernel(distances, ranges, conv_ref, down_ref, second_ref, *first_refs):
    row = lax.broadcasted_iota(jnp.int32, (2 * C, 2 * C), 0)
    lane = lax.broadcasted_iota(jnp.int32, (2 * C, 2 * C), 1)
    hidden = 2 * lax.rem(lane, C // 2) + lax.div(lax.rem(lane, C), C // 2)
    pair = [
        [((row == C * odd + hidden) & (lax.div(lane, C) == k)).astype(jnp.bfloat16) for k in range(2)]
        for odd in range(2)
    ]
    in_order = (row == 2 * lax.rem(lane, C) + lax.div(lane, C)).astype(jnp.bfloat16)
    down = [[down_ref[a, b].reshape(3, C, 2 * C) for b in range(3)] for a in range(3)]
    for j in range(14):
        halves = []
        for odd in range(2):
            total = None
            for k in range(2):
                t = 2 * j + k
                if t < 27:
                    part = exact(down[t // 3 % 3][t // 9][t % 3], pair[odd][k])
                    total = part if total is None else total + part
            halves.append(total.astype(jnp.bfloat16))
        second_ref[:, pl.ds(2 * C * j, 2 * C)] = exact(in_order, jnp.concatenate(halves)).astype(jnp.bfloat16)
    conv = [[conv_ref[a, b].reshape(3, C // 2, 2 * C) for b in range(3)] for a in range(3)]
    taps = [[jnp.concatenate([conv[a][b][c] for a in range(3)]) for c in range(3)] for b in range(3)]
    for (start, channels), first_ref in zip(ranges, first_refs):
        row = lax.broadcasted_iota(jnp.int32, (2 * C, 12 * channels), 0)
        lane = lax.broadcasted_iota(jnp.int32, (2 * C, 12 * channels), 1)
        place = start + lax.rem(lane, channels)
        source = place
        if distances:
            me, count = lax.axis_index("filt"), C // len(distances)
            for i, d in enumerate(distances):
                moved = lax.bitwise_xor(me, d) * count + place - i * count
                source = jnp.where(lax.div(place, count) == i, moved, source)
        for odd in range(2):
            shift = jnp.where(row == C * odd + source, lax.div(lane, channels), -1)
            for parity in range(2):
                total = None
                for b in range(3):
                    for c in range(3):
                        part = exact(taps[b][c], (shift == 4 * b + c + parity).astype(jnp.bfloat16))
                        total = part if total is None else total + part
                total = total.astype(jnp.bfloat16)
                for a in range(3):
                    at = (2 - a) * 2 * C + parity * C + odd * C // 2
                    first_ref[pl.ds(at, C // 2), :] = total[a * C // 2 : (a + 1) * C // 2]


def swapped(block, axis, *others):
    count = lax.axis_size(axis)
    results = []
    for start in (1, 0):
        pairs = [(i, i + 1) for i in range(start, count - 1, 2)]
        if start == 0 and others:
            block = after(block, *others)
        results.append(lax.ppermute(block, axis, pairs + [(j, i) for i, j in pairs]))
    return results


def after(value, *others):
    return lax.optimization_barrier((value, *others))[0]


def in_vmem(value):
    return pltpu.with_memory_space_constraint(value, pltpu.VMEM)


def local(volume, conv_weight, down_weight):
    bands = lax.axis_size("filt")
    count, planes, all_rows, width = volume.shape
    band = all_rows // bands
    window = BELOW + band + ABOVE
    half = width // 2
    hid_rows = band + 1
    vmem = pl.BlockSpec(memory_space=pltpu.VMEM)
    params = pltpu.CompilerParams(vmem_limit_bytes=VMEM_LIMIT)
    cost = pl.CostEstimate(flops=1, transcendentals=0, bytes_accessed=1)
    direct = count == 16 and bands == 4
    distances = (0, 2, 1, 3) if direct else ()
    ranges = [(0, 48), (0, 16), (16, 32), (48, 16)] if direct else [(0, C)]
    lay = pl.pallas_call(
        functools.partial(weight_kernel, distances, ranges),
        out_shape=[pltpu.VMEM((C2, 28 * C), jnp.bfloat16)]
        + [pltpu.VMEM((6 * C, 12 * channels), jnp.bfloat16) for _, channels in ranges],
        in_specs=[vmem] * 2,
        out_specs=[vmem] * (1 + len(ranges)),
        compiler_params=params,
        cost_estimate=cost,
    )
    def convolve(feature, groups, second=None):
        arrays = [] if feature is None else [feature]
        last = second is not None
        arrays += [second] if last else []
        for _, *given in groups:
            arrays += given
        kinds = [group for group, *_ in groups]
        scratch = [pltpu.VMEM((hid_rows * 9 * C, half), jnp.bfloat16)] * last
        for group in kinds:
            slots = 2 if group.inside else 4
            scratch.append(pltpu.VMEM((slots, window * 4 * group.channels, half), jnp.bfloat16))
        if last:
            shape = pltpu.VMEM((band // 2, C2, half), jnp.bfloat16)
        else:
            shape = pltpu.VMEM((hid_rows * 6 * C, half), jnp.float32)
        return pl.pallas_call(
            functools.partial(conv_kernel, kinds, window, feature is None, last),
            out_shape=shape,
            in_specs=[vmem] * len(arrays),
            out_specs=vmem,
            scratch_shapes=scratch,
            compiler_params=params,
            cost_estimate=pl.CostEstimate(flops=1 << 33, transcendentals=0, bytes_accessed=1 << 24),
        )(*map(in_vmem, arrays))

    if direct:
        step = 16
        cut = (window + 1) // 2
        sends = [(d, 0, window) for d in distances[:3]] + [(distances[3], 0, cut), (distances[3], cut, window)]
        sent = pl.pallas_call(
            functools.partial(send_kernel, band, sends),
            out_shape=[
                jax.ShapeDtypeStruct((high - low, planes, count, width), jnp.bfloat16)
                for _, low, high in sends
            ],
            in_specs=[pl.BlockSpec(memory_space=pltpu.HBM)],
            out_specs=[vmem] * len(sends),
            scratch_shapes=[
                pltpu.VMEM((planes * all_rows // step, count, step, width), jnp.bfloat16),
                pltpu.VMEM((BELOW + all_rows + ABOVE, planes, count, width), jnp.bfloat16),
                pltpu.SemaphoreType.DMA((planes * all_rows // step,)),
            ],
            compiler_params=params,
            cost_estimate=cost,
        )(pltpu.with_memory_space_constraint(volume, pltpu.HBM))
        second, *firsts = lay(
            pltpu.with_memory_space_constraint(conv_weight, pltpu.HBM),
            pltpu.with_memory_space_constraint(down_weight, pltpu.HBM),
        )
        own = []
        for (d, _, _), piece in zip(sends, sent):
            if d:
                piece = lax.ppermute(piece, "filt", [(i, i ^ d) for i in range(bands)])
            own.append(piece)
        mine = swapped(after(own[0], firsts[0]), "space")
        middle = pl.pallas_call(
            join_kernel,
            out_shape=pltpu.VMEM((2 * window, planes, count, width), jnp.bfloat16),
            in_specs=[vmem] * 2,
            out_specs=vmem,
            compiler_params=params,
            cost_estimate=cost,
        )(*map(in_vmem, own[1:3]))
        middles = swapped(middle, "space", *mine)
        all_three, of_own, of_middle, of_last = firsts
        full = (0, window)
        feature = convolve(
            None,
            [
                (
                    Group(True, 48, [(0, 0, 0, *full), (1, 0, 16, *full), (1, window, 32, *full)]),
                    all_three,
                    own[0],
                    middle,
                ),
                (Group(False, 16, [(0, 0, 0, *full), (1, 0, 0, *full)]), of_own, *mine),
            ],
        )
        heads = swapped(after(own[3], feature), "space")
        tails = swapped(after(own[4], feature), "space")
        middles = [after(block, own[4]) for block in middles]
        in_middle = [(i, at * window, at * 16, *full) for i in range(2) for at in range(2)]
        halves = ((0, cut), (cut, window))
        feature = convolve(
            feature,
            [
                (Group(True, 16, [(i, 0, 0, *halves[i]) for i in range(2)]), of_last, own[3], own[4]),
                (Group(False, 32, in_middle), of_middle, *middles),
            ],
        )
        in_last = [(i, 0, 0, *halves[i // 2]) for i in range(4)]
        coarse = convolve(feature, [(Group(False, 16, in_last), of_last, *heads, *tails)], second)
    else:
        field = jnp.transpose(volume, (2, 1, 0, 3))
        field = jnp.concatenate([field[..., ::2], field[..., 1::2]], axis=-1)
        field = jnp.pad(field, ((BELOW, ABOVE), (0, 0), (0, 0), (0, 0)))
        sent = jnp.stack([field[t * band : t * band + window] for t in range(bands)])
        got = lax.all_to_all(sent, "filt", split_axis=0, concat_axis=0, tiled=True)
        own = jnp.transpose(got, (1, 2, 0, 3, 4)).reshape(window, planes, C, width)
        second, *firsts = lay(conv_weight, down_weight)
        inside = (Group(True, C, [(0, 0, 0, 0, window)]), firsts[0], own)
        outside = (Group(False, C, [(0, 0, 0, 0, window), (1, 0, 0, 0, window)]), firsts[0], *swapped(own, "space"))
        coarse = convolve(None, [inside, outside], second)
    return jnp.transpose(coarse, (1, 0, 2))[:, None]


def solution(mesh):
    return jax.shard_map(
        local,
        mesh=mesh,
        in_specs=(P("filt", ("groups", "space"), None, None), P(), P()),
        out_specs=P(None, ("groups", "space"), "filt", None),
        check_vma=False,
    )
```
